32 devices in a mesh: groups: 2 (over x), dp: 4 (over y, core), tensor: 4 (over z).
Axes of the slice: x: 2, y: 2, z: 4, core: 2. Of those that a mesh axis runs over, the one named last changes fastest.
Arguments:
- hidden: bfloat16 [4096, 8192], P(('groups', 'dp'), 'tensor'), parts along dimension 0, may hold values from -0.59765625 to 0.59765625
- query_gradient: bfloat16 [4096, 4096], P(('groups', 'dp'), 'tensor'), parts along dimension 0, may hold values from -6 to 6
- frozen_query_weight: bfloat16 [8192, 4096], P(None, 'tensor'), may hold values from -0.0625 to 0.0625
- adapter_down_weight: bfloat16 [16, 8192, 64], P(('groups', 'dp'), 'tensor'), parts along dimension 0, may hold values from -0.0625 to 0.0625
- adapter_up_weight: bfloat16 [16, 64, 4096], P(('groups', 'dp'), None, 'tensor'), parts along dimension 0, may hold values from -0.09375 to 0.09375
- block_member_owner: int32 [32], P('groups'), parts along dimension 0, may hold values from 0 to 7, as said below
- member_last_block_count: int32 [16], P('groups'), parts along dimension 0, may hold values from 1 to 128
Outputs:
- hidden_gradient: bfloat16 [4096, 8192], P(('groups', 'dp'), 'tensor'), parts along dimension 0
- grad_down: float32 [16, 8192, 64], P(('groups', 'dp'), 'tensor'), parts along dimension 0
- grad_up: float32 [16, 64, 4096], P(('groups', 'dp'), None, 'tensor'), parts along dimension 0
The draws below stay inside these ranges and needn't reach their ends.
There are 2 independent parts, one for each index of `groups`. The reference program is written for one: setup_inputs(seed, part) draws one part's arguments, and reference() takes and returns one part's arrays. A program takes and returns all parts, laid end to end along the dimension named above; an argument that names none is the same for every part. Nothing has to cross between parts.
Inputs may be any that keep to these rules, and one draw needn't show every extreme that they name: `block_member_owner`: the blocks come in consecutive runs, one run for each member, in an order drawn from the seed; each run is 1 to 3 blocks long, and at least one run is exactly 3 blocks long.
All inputs are finite; a program needn't handle non-finite values.
Results may differ from the reference program's by a relative error of at most 0.015.
Values may be sent and summed in bfloat16 or wider, within the bound.
No kernel may reach another device: no remote copies, remote signals or barrier semaphores. Data moves between devices by JAX's collectives and lax.ppermute only.
A program may use at most 128 MiB of HBM per device.

```python
import jax
import jax.numpy as jnp
from jax import lax

MODEL_WIDTH = 8192
HEAD = 128
HEADS = 32
ADAPTER_RANK = 64
BLK = 128
BLK_DEV = 4
QUERY_FEATURES = 4096
LEAGUE_MEMBERS = 8
BLOCKS = 16
TOKENS = 2048
N_DP = 4
N_TENSOR = 4


def draw_block_member_owner(key, part):
    key = jax.random.fold_in(key, 11)
    key_first, key_pick, key_flip, key_order = jax.random.split(key, 4)
    average = BLOCKS // LEAGUE_MEMBERS
    pairs = LEAGUE_MEMBERS // 2
    first = jax.random.randint(key_first, (pairs,), 1, 2 * average, dtype=jnp.int32)
    special = jax.random.randint(key_pick, (), 0, pairs, dtype=jnp.int32)
    first = jnp.where(jnp.arange(pairs, dtype=jnp.int32) == special, 2 * average - 1, first)
    flips = jax.random.randint(key_flip, (pairs,), 0, 2, dtype=jnp.int32)
    left = jnp.where(flips == 1, first, 2 * average - first)
    right = 2 * average - left
    lengths = jnp.stack([left, right], axis=1).reshape(-1)
    ends = jnp.cumsum(lengths).astype(jnp.int32)
    places = jnp.arange(BLOCKS, dtype=jnp.int32)
    run_index = jnp.sum((ends[None, :] <= places[:, None]).astype(jnp.int32), axis=1)
    order = jax.random.permutation(key_order, jnp.arange(LEAGUE_MEMBERS, dtype=jnp.int32))
    return jnp.take(order, run_index).astype(jnp.int32)


def place_ends(values, key, least, largest):
    shape = values.shape
    index_at = [jax.random.randint(jax.random.fold_in(key, axis), (), 0, shape[axis]) for axis in range(len(shape))]
    values = values.at[tuple(index_at)].set(least)
    longest = shape.index(max(shape))
    index_at[longest] = (index_at[longest] + 1) % shape[longest]
    return values.at[tuple(index_at)].set(largest)


def block_scale(rng, dims, cuts, low, top_value):
    def one(position, blocks):
        draws = jax.random.uniform(jax.random.fold_in(jax.random.fold_in(rng, 6), position), (blocks,), jnp.float32, low / len(cuts), top_value / len(cuts))
        return jnp.repeat(jnp.exp(draws), dims[position] // blocks).reshape((-1,) + (1,) * (len(dims) - position - 1))

    loudness = one(*cuts[0])
    for cut in cuts[1:]:
        loudness = loudness * one(*cut)
    return loudness


def noise(rng, shape, deviation, most, cuts=(), kind=jnp.bfloat16):
    values = jax.random.normal(rng, shape, jnp.float32) * deviation
    if len(cuts) > 0:
        values = block_scale(rng, shape, cuts, -0.22, 0.18) * values
    return jnp.clip(values, min=-most, max=most).astype(kind)


def setup_inputs(seed: int = 0, part: int = 0) -> dict:
    splits = jax.random.split(jax.random.key(seed), 8)
    own_keys = jax.random.split(jax.random.fold_in(splits[7], part), 8)
    hidden = noise(own_keys[0], (TOKENS, MODEL_WIDTH), 0.1, 0.59765625, ((0, 4), (1, 4)))
    query_gradient = noise(own_keys[1], (TOKENS, QUERY_FEATURES), 1.0, 6.0, ((0, 4), (1, 4)))
    frozen_query_weight = noise(splits[2], (MODEL_WIDTH, QUERY_FEATURES), MODEL_WIDTH ** -0.5, 0.0625, ((1, 4),))
    adapter_down_weight = noise(own_keys[3], (LEAGUE_MEMBERS, MODEL_WIDTH, ADAPTER_RANK), MODEL_WIDTH ** -0.5, 0.0625, ((0, 4), (1, 4)))
    adapter_up_weight = noise(own_keys[4], (LEAGUE_MEMBERS, ADAPTER_RANK, QUERY_FEATURES), QUERY_FEATURES ** -0.5, 0.09375, ((0, 4), (2, 4)))
    block_member_owner = draw_block_member_owner(jax.random.fold_in(jax.random.fold_in(splits[7], part), 71), part)
    member_last_block_count = place_ends(jax.random.randint(own_keys[6], (LEAGUE_MEMBERS,), 1, BLK + 1), jax.random.fold_in(own_keys[6], 1), 1, BLK).astype(jnp.int32)
    return {"hidden": hidden, "query_gradient": query_gradient, "frozen_query_weight": frozen_query_weight, "adapter_down_weight": adapter_down_weight, "adapter_up_weight": adapter_up_weight, "block_member_owner": block_member_owner, "member_last_block_count": member_last_block_count}


def live_mask(block_member_owner, member_last_block_count):
    following = jnp.concatenate([block_member_owner[1:], jnp.full((1,), -1, jnp.int32)])
    closing = block_member_owner != following
    tails = jnp.take(member_last_block_count, block_member_owner)
    places = jnp.arange(BLK, dtype=jnp.int32)
    return jnp.logical_or(jnp.logical_not(closing)[:, None], places[None, :] < tails[:, None])


def reference(hidden, query_gradient, frozen_query_weight, adapter_down_weight, adapter_up_weight, block_member_owner, member_last_block_count):
    width_q = HEADS * HEAD
    group_cols = width_q // N_TENSOR
    live = live_mask(block_member_owner, member_last_block_count)
    member_ids = jnp.arange(LEAGUE_MEMBERS, dtype=jnp.int32)

    def device_step(carry, index):
        down_acc, up_acc = carry
        first = index * BLK_DEV
        member_list = lax.dynamic_slice_in_dim(block_member_owner, first, BLK_DEV)
        token_rows = lax.dynamic_slice_in_dim(hidden, first * BLK, BLK_DEV * BLK)
        cotan = lax.dynamic_slice_in_dim(query_gradient, first * BLK, BLK_DEV * BLK)
        keep = lax.dynamic_slice_in_dim(live, first, BLK_DEV).reshape(-1)
        cotan = jnp.where(keep[:, None], cotan, jnp.zeros_like(cotan))
        token_rows_float = token_rows.astype(jnp.float32).reshape(BLK_DEV, BLK, MODEL_WIDTH)
        cotan_f = cotan.astype(jnp.float32).reshape(BLK_DEV, BLK, width_q)
        selected_down = jnp.take(adapter_down_weight, member_list, axis=0).astype(jnp.float32)
        selected_up = jnp.take(adapter_up_weight, member_list, axis=0).astype(jnp.float32)
        rank_activation = jnp.einsum("nhx,nxs->nhs", token_rows_float, selected_down).astype(jnp.bfloat16)
        rank_gradient = jnp.einsum("bkq,brq->bkr", cotan_f, selected_up).astype(jnp.bfloat16)
        frozen_term = jnp.zeros((BLK_DEV * BLK, MODEL_WIDTH), jnp.float32)
        for group in range(N_TENSOR):
            part = jnp.dot(cotan[:, group * group_cols:(group + 1) * group_cols],
                           frozen_query_weight[:, group * group_cols:(group + 1) * group_cols].T,
                           preferred_element_type=jnp.float32)
            part = lax.optimization_barrier(part.astype(jnp.bfloat16))
            frozen_term = frozen_term + part.astype(jnp.float32)
        adapter_contribution = jnp.einsum("jym,jim->jyi", rank_gradient.astype(jnp.float32), selected_down).reshape(-1, MODEL_WIDTH)
        gradient_row_block = (frozen_term + adapter_contribution).astype(jnp.bfloat16)
        onehot = (member_ids[:, None] == member_list[None, :]).astype(jnp.float32)
        block_down_matrix = jnp.einsum("uza,uzm->uam", token_rows_float, rank_gradient.astype(jnp.float32))
        share_down = jnp.einsum("mb,bdr->mdr", onehot, block_down_matrix)
        share_down = lax.optimization_barrier(share_down.astype(jnp.bfloat16))
        block_up = jnp.einsum("bkr,bkq->brq", rank_activation.astype(jnp.float32), cotan_f)
        share_up = jnp.einsum("mb,brq->mrq", onehot, block_up)
        share_up = lax.optimization_barrier(share_up.astype(jnp.bfloat16))
        return (down_acc + share_down.astype(jnp.float32), up_acc + share_up.astype(jnp.float32)), gradient_row_block

    start = (jnp.zeros((LEAGUE_MEMBERS, MODEL_WIDTH, ADAPTER_RANK), jnp.float32), jnp.zeros((LEAGUE_MEMBERS, ADAPTER_RANK, width_q), jnp.float32))
    (grad_down, grad_up), gradient_row_block = lax.scan(device_step, start, jnp.arange(N_DP, dtype=jnp.int32))
    hidden_gradient = gradient_row_block.reshape(TOKENS, MODEL_WIDTH)
    return hidden_gradient, grad_down, grad_up
```

```python
import jax
import jax.numpy as jnp
from jax import lax
from jax.sharding import PartitionSpec as P

BLK = 128
BF = jnp.bfloat16
F32 = jnp.float32


def live_mask(owner, counts):
    following = jnp.concatenate([owner[1:], jnp.full((1,), -1, jnp.int32)])
    closing = owner != following
    tails = jnp.take(counts, owner)
    places = jnp.arange(BLK, dtype=jnp.int32)
    return jnp.logical_or(jnp.logical_not(closing)[:, None], places[None, :] < tails[:, None])


def swap(a, axis, size, bit):
    return lax.ppermute(a, axis, [(i, i ^ (1 << bit)) for i in range(size)])


def body(hidden, query_gradient, weight, down, up, owner, counts):
    n = lax.axis_size("tensor")
    nd = lax.axis_size("dp")
    ng = lax.axis_size("groups")
    z = lax.axis_index("tensor")
    me = lax.axis_index("dp")
    width = hidden.shape[1]
    cols = query_gradient.shape[1]
    tokens = hidden.shape[0]
    blocks = tokens // BLK
    owned = down.shape[0]
    rank = down.shape[2]
    share = width // (ng * nd)
    place = lax.axis_index("groups") * nd + me

    ups, downs = [], []
    a = b = query_gradient
    for r in range(1, n):
        a = lax.ppermute(a, "tensor", [(i, i + 1) for i in range(r - 1, n - 1)])
        b = lax.ppermute(b, "tensor", [(i, i - 1) for i in range(n - r, 0, -1)])
        ups.append(a)
        downs.append(b)
    wide = []
    for step in range(1, n):
        to = lax.rem(z + step, n)
        piece = lax.dynamic_slice(weight, (to * width + place * share, 0), (share, cols))
        piece = lax.ppermute(piece, "tensor", [(i, (i + step) % n) for i in range(n)])
        wide.append(lax.all_gather(piece, ("groups", "dp"), axis=0, tiled=True))

    bits = list(range(nd.bit_length() - 2, -1, -1))
    table = jnp.concatenate([jnp.swapaxes(down, 1, 2), up], axis=2)
    for bit in bits:
        table = jnp.concatenate([table, swap(table, "dp", nd, bit)], axis=0)
    first = me * blocks
    members = lax.dynamic_slice_in_dim(owner, first, blocks)
    keep = lax.dynamic_slice_in_dim(live_mask(owner, counts), first, blocks).reshape(-1)
    relative = (members // owned) ^ me
    slot = members % owned
    for j, bit in enumerate(bits):
        slot = slot + (((relative >> bit) & 1) << j) * owned
    chosen = jnp.take(table, slot, axis=0)
    chosen_down, chosen_up = chosen[:, :, :width], chosen[:, :, width:]

    hid = hidden.reshape(blocks, BLK, width)
    cot = query_gradient.reshape(blocks, BLK, cols)
    act = jnp.einsum("bth,brh->btr", hid, chosen_down, preferred_element_type=F32)
    grad = jnp.einsum("btq,brq->btr", cot, chosen_up, preferred_element_type=F32)
    both = jnp.concatenate([act, grad], axis=2).astype(BF)
    for bit in range(n.bit_length() - 1):
        both = (both.astype(F32) + swap(both, "tensor", n, bit).astype(F32)).astype(BF)
    both = jnp.where(keep.reshape(blocks, BLK, 1), both, jnp.zeros_like(both))
    rank_act, rank_grad = both[:, :, :rank], both[:, :, rank:]

    block_down = jnp.einsum("btr,bth->brh", rank_grad, hid, preferred_element_type=F32)
    block_up = jnp.einsum("btr,btq->brq", rank_act, cot, preferred_element_type=F32)
    onehot = (jnp.arange(nd * owned, dtype=jnp.int32)[:, None] == slot[None, :]).astype(F32)
    total = jnp.concatenate(
        [
            jnp.einsum("mb,brh->mrh", onehot, block_down),
            jnp.einsum("mb,brq->mrq", onehot, block_up),
        ],
        axis=2,
    ).astype(BF)
    for bit in reversed(bits):
        half = total.shape[0] // 2
        got = swap(total[half:], "dp", nd, bit)
        total = total[:half].astype(F32) + got.astype(F32)
        if bit != bits[0]:
            total = total.astype(BF)
    grad_down = jnp.swapaxes(total[:, :, :width], 1, 2)
    grad_up = total[:, :, width:]

    def dot(c, w):
        return lax.dot_general(c, w, (((1,), (1,)), ((), ())), preferred_element_type=F32)

    result = dot(query_gradient, lax.dynamic_slice_in_dim(weight, z * width, width, 0))
    for step in range(1, n):
        c = jnp.where(z >= step, ups[step - 1], downs[n - step - 1])
        result = result + dot(c, wide[step - 1])
    result = jnp.where(keep[:, None], result, 0.0)
    extra = jnp.einsum("btr,brh->bth", rank_grad, chosen_down, preferred_element_type=F32)
    result = result + extra.reshape(tokens, width)
    return result.astype(BF), grad_down, grad_up


def solution(mesh):
    return jax.shard_map(
        body,
        mesh=mesh,
        in_specs=(
            P(("groups", "dp"), "tensor"),
            P(("groups", "dp"), "tensor"),
            P(None, "tensor"),
            P(("groups", "dp"), "tensor", None),
            P(("groups", "dp"), None, "tensor"),
            P("groups"),
            P("groups"),
        ),
        out_specs=(
            P(("groups", "dp"), "tensor"),
            P(("groups", "dp"), "tensor", None),
            P(("groups", "dp"), None, "tensor"),
        ),
        check_vma=False,
    )
```

```python
import functools

import jax
import jax.numpy as jnp
from jax import lax
from jax.experimental import pallas as pl
from jax.experimental.pallas import tpu as pltpu
from jax.sharding import PartitionSpec as P

BLK = 128
PIECE = 256
TILE = 2 * PIECE
BF = jnp.bfloat16
F32 = jnp.float32
VMEM_LIMIT = 56 * 2**20


CHEAP = pl.CostEstimate(flops=1, bytes_accessed=1, transcendentals=0)


def move(name, a, axis, pairs):
    with jax.named_scope(name):
        return lax.ppermute(a, axis, pairs)


def swap(name, a, axis, size, bit):
    return move(name, a, axis, [(i, i ^ (1 << bit)) for i in range(size)])


def together(*values):
    return lax.optimization_barrier(values)


def contract_last(a, b):
    return lax.dot_general(a, b, (((1,), (1,)), ((), ())), preferred_element_type=F32)


def contract_first(a, b):
    return lax.dot_general(a, b, (((0,), (0,)), ((), ())), preferred_element_type=F32)


def params():
    return pltpu.CompilerParams(vmem_limit_bytes=VMEM_LIMIT)


def slot_of(block, ids, owner, *, blocks, owned, bits):
    member = owner[ids[1] * blocks + block]
    relative = (member // owned) ^ ids[1]
    slot = member % owned
    for j, bit in enumerate(bits):
        slot = slot + ((relative >> bit) & 1) * (owned << j)
    return slot


def live_count(block, ids, owner, counts, *, blocks):
    at = ids[1] * blocks + block
    last = owner.shape[0] - 1
    member = owner[at]
    closing = jnp.logical_or(at == last, owner[jnp.minimum(at + 1, last)] != member)
    return jnp.where(closing, counts[member], BLK)


def rank_kernel(ids, owner, counts, hid, cot, *refs, width, blocks, slot, held):
    b = pl.program_id(0)
    count = live_count(b, ids, owner, counts, blocks=blocks)
    parts, out = refs[:-1], refs[-1]
    for i, part in enumerate(parts):

        @pl.when(slot(b, ids, owner) // held == i)
        def _(part=part):
            act = contract_last(hid[...], part[0, :, :width])
            grad = contract_last(cot[...], part[0, :, width:])
            both = jnp.concatenate([act, grad], axis=1)
            rows = lax.broadcasted_iota(jnp.int32, both.shape, 0)
            out[...] = jnp.where(rows < count, both, 0.0).astype(BF)


def rank_partials(ids, owner, counts, hidden, cotan, table, *, blocks, owned, bits):
    width, cols = hidden.shape[1], cotan.shape[1]
    held, rank = table[0].shape[:2]
    slot = functools.partial(slot_of, blocks=blocks, owned=owned, bits=bits)

    def chosen(i):
        def index(b, ids, owner, counts):
            at = slot(b, ids, owner)
            return (jnp.where(at // held == i, at % held, 0), 0, 0)

        return pl.BlockSpec((1, rank, width + cols), index)

    return pl.pallas_call(
        functools.partial(rank_kernel, width=width, blocks=blocks, slot=slot, held=held),
        grid_spec=pltpu.PrefetchScalarGridSpec(
            num_scalar_prefetch=3,
            grid=(blocks,),
            in_specs=[
                pl.BlockSpec((BLK, width), lambda b, *s: (b, 0)),
                pl.BlockSpec((BLK, cols), lambda b, *s: (b, 0)),
            ]
            + [chosen(i) for i in range(len(table))],
            out_specs=pl.BlockSpec((BLK, 2 * rank), lambda b, *s: (b, 0)),
        ),
        out_shape=jax.ShapeDtypeStruct((blocks * BLK, 2 * rank), BF),
        compiler_params=params(),
        cost_estimate=CHEAP,
        name="rank_partials",
    )(ids, owner, counts, hidden, cotan, *table)


def grads_kernel(ids, owner, hid, cot, both, send, keep, acc, *, width, blocks, slot, half):
    step = pl.program_id(0)
    position = jnp.where(step < half, step + half, step - half)
    rank = both.shape[1] // 2
    acc[...] = jnp.zeros_like(acc)
    for b in range(blocks):

        @pl.when(slot(b, ids, owner) == position)
        def _(b=b):
            at = pl.ds(b * BLK, BLK)
            pair = both[at, :].astype(F32)
            acc[:, :width] += contract_first(pair[:, rank:].astype(BF), hid[at, :])
            acc[:, width:] += contract_first(pair[:, :rank].astype(BF), cot[at, :])

    @pl.when(step < half)
    def _():
        send[0] = acc[...].astype(BF)

    @pl.when(step >= half)
    def _():
        keep[0] = acc[...].astype(BF)


def member_grads(ids, owner, hidden, cotan, both, members, *, blocks, owned, bits):
    tokens, width = hidden.shape
    cols = cotan.shape[1]
    rank = both.shape[1] // 2
    half = members // 2
    slot = functools.partial(slot_of, blocks=blocks, owned=owned, bits=bits)
    shape = jax.ShapeDtypeStruct((half, rank, width + cols), BF)
    return pl.pallas_call(
        functools.partial(
            grads_kernel, width=width, blocks=blocks, slot=slot, half=half
        ),
        grid_spec=pltpu.PrefetchScalarGridSpec(
            num_scalar_prefetch=2,
            grid=(members,),
            in_specs=[
                pl.BlockSpec((tokens, width), lambda p, *s: (0, 0)),
                pl.BlockSpec((tokens, cols), lambda p, *s: (0, 0)),
                pl.BlockSpec((tokens, 2 * rank), lambda p, *s: (0, 0)),
            ],
            out_specs=[
                pl.BlockSpec((1, rank, width + cols), lambda p, *s: (jnp.minimum(p, half - 1), 0, 0)),
                pl.BlockSpec((1, rank, width + cols), lambda p, *s: (jnp.maximum(p - half, 0), 0, 0)),
            ],
            scratch_shapes=[pltpu.VMEM((rank, width + cols), F32)],
        ),
        out_shape=[shape, shape],
        compiler_params=params(),
        cost_estimate=CHEAP,
        name="member_grads",
    )(ids, owner, hidden, cotan, both)


def relative_tile(p, ids):
    core = (ids[1] & 1) ^ (p >> 1)
    x, y = ids[0], (ids[1] >> 1) & 1
    at = jnp.where(core == 0, y ^ (p & 1), 2 + (x ^ (p & 1)))
    return at, jnp.where(core == 0, x, y)


def plain_tile(p, ids):
    return p, 0


def tile_part(half, flip):
    return pl.ds(pl.multiple_of((half ^ flip) * PIECE, PIECE), PIECE)


def by_part(p, parts, run):
    if parts == 1:
        run(0)
        return
    for i in range(parts):
        pl.when(p == i)(functools.partial(run, i))


def local_kernel(ids, cot, weight, out):
    out[...] = contract_last(cot[...], weight[...])


def local_products(ids, cotan, weight, width):
    tokens, cols = cotan.shape
    tiles = width // TILE
    return pl.pallas_call(
        local_kernel,
        grid_spec=pltpu.PrefetchScalarGridSpec(
            num_scalar_prefetch=1,
            grid=(tiles,),
            in_specs=[
                pl.BlockSpec((tokens, cols), lambda p, *s: (0, 0)),
                pl.BlockSpec((TILE, cols), lambda p, i: (i[2] * tiles + p, 0)),
            ],
            out_specs=pl.BlockSpec((tokens, TILE), lambda p, *s: (0, p)),
        ),
        out_shape=jax.ShapeDtypeStruct((tokens, width), F32),
        compiler_params=params(),
        cost_estimate=CHEAP,
        name="local_products",
    )(ids, cotan, weight)


def fold_kernel(ids, owner, counts, acc, *refs, terms, parts, tile, first, blocks, slot, table_parts, held, final):
    p = pl.program_id(0)
    xs, refs = refs[:terms], refs[terms:]
    ws, refs = refs[: terms * parts], refs[terms * parts :]
    table, out = refs[:table_parts], refs[-1]
    _, flip = tile(first + p, ids)
    rows = lax.broadcasted_iota(jnp.int32, (BLK, PIECE), 0)

    def run(i):
        total = contract_last(xs[0][...], ws[i][...])
        for t in range(1, terms):
            total += contract_last(xs[t][...], ws[t * parts + i][...])
        for half in range(2):
            to = tile_part(half, flip)
            part = acc[:, to] + total[:, half * PIECE : (half + 1) * PIECE]
            if not final:
                out[:, to] = part
                continue
            for b in range(blocks):
                at = slice(b * BLK, (b + 1) * BLK)
                count = live_count(b, ids, owner, counts, blocks=blocks)
                out[at, to] = jnp.where(rows < count, part[at], 0.0).astype(BF)

    by_part(p, parts, run)
    if table:
        both = refs[table_parts]
        rank = both.shape[1] // 2
        for b in range(blocks):
            at = slice(b * BLK, (b + 1) * BLK)
            place = slot(b, ids, owner)
            for i, part in enumerate(table):

                @pl.when(place // held == i)
                def _(at=at, place=place, part=part):
                    out[at, :] += lax.dot_general(
                        both[at, rank:],
                        part[place % held],
                        (((1,), (0,)), ((), ())),
                        preferred_element_type=F32,
                    )


def fold(ids, owner, counts, acc, xs, ws, tile, first, *, blocks, owned, bits, before=None, final=False, table=(), both=None):
    tokens, width = acc.shape
    cols = xs[0].shape[1]
    parts = len(ws[0])
    flat = [part for w in ws for part in w]
    tiles = parts if parts > 1 else flat[0].shape[0] // TILE
    slot = functools.partial(slot_of, blocks=blocks, owned=owned, bits=bits)
    block = pl.BlockSpec((tokens, TILE), lambda p, i, *s: (0, tile(first + p, i)[0]))
    operands = [ids, owner, counts, acc, *xs, *flat, *table]
    in_specs = [block]
    in_specs += [pl.BlockSpec((tokens, cols), lambda p, *s: (0, 0)) for _ in xs]
    in_specs += [pl.BlockSpec((TILE, cols), lambda p, *s: (p if parts == 1 else 0, 0)) for _ in flat]
    held = 0
    if table:
        held, rank = table[0].shape[:2]
        in_specs += [
            pl.BlockSpec((held, rank, TILE), lambda p, i, *s: (0, 0, tile(first + p, i)[0])) for _ in table
        ]
        operands.append(both)
        in_specs.append(pl.BlockSpec((tokens, 2 * rank), lambda p, *s: (0, 0)))
    alias = {} if final else {3: 0}
    if before is not None:
        alias = {len(operands): 0}
        operands.append(before)
        in_specs.append(pl.BlockSpec(memory_space=pl.ANY))
    return pl.pallas_call(
        functools.partial(
            fold_kernel,
            terms=len(xs),
            parts=parts,
            tile=tile,
            first=first,
            blocks=blocks,
            slot=slot,
            table_parts=len(table),
            held=held,
            final=final,
        ),
        grid_spec=pltpu.PrefetchScalarGridSpec(
            num_scalar_prefetch=3, grid=(tiles,), in_specs=in_specs, out_specs=block
        ),
        out_shape=jax.ShapeDtypeStruct((tokens, width), BF if final else F32),
        input_output_aliases=alias,
        compiler_params=params(),
        cost_estimate=CHEAP,
        name="finish" if final else "fold",
    )(*operands)


def line(cotan, n, z):
    ups, downs = [], []
    a = b = cotan
    for r in range(1, n):
        a = lax.ppermute(a, "tensor", [(i, i + 1) for i in range(r - 1, n - 1)])
        b = lax.ppermute(b, "tensor", [(i, i - 1) for i in range(n - r, 0, -1)])
        ups.append(a)
        downs.append(b)
    return [jnp.where(z >= s, ups[s - 1], downs[n - s - 1]) for s in range(1, n)]


def body(hidden, query_gradient, weight, down, up, owner, counts):
    n = lax.axis_size("tensor")
    nd = lax.axis_size("dp")
    ng = lax.axis_size("groups")
    x, me, z = lax.axis_index("groups"), lax.axis_index("dp"), lax.axis_index("tensor")
    middle = jnp.logical_and(z > 0, z < n - 1)
    ids = jnp.stack([x, me, z, middle.astype(jnp.int32)]).astype(jnp.int32)
    tokens, width = hidden.shape
    cols = query_gradient.shape[1]
    owned = down.shape[0]
    share = width // (ng * nd)
    bits = tuple(range(nd.bit_length() - 2, -1, -1))
    half = tokens // 2
    sizes = dict(blocks=tokens // BLK, owned=owned, bits=bits)
    fast = (ng, nd, n, share) == (2, 4, 4, PIECE)

    if fast:
        y, core = me // 2, me % 2
        place = jnp.where(core == 0, 2 * y + x, 4 + 2 * x + y)
        turn_a = [(i, i ^ (4 if i % 2 == 0 else 2)) for i in range(8)]
        turn_b = [(i, i ^ (2 if i % 2 == 0 else 4)) for i in range(8)]
        turn_c = [(i, i ^ 1) for i in range(8)]
        outer, inner = [(0, 1), (1, 0), (2, 3), (3, 2)], [(1, 2), (2, 1)]
        outward = [(1, 0), (2, 3)]
    else:
        place = x * nd + me
    copies = ("groups", "dp")

    def cut(to):
        return lax.dynamic_slice(weight, (to * width + place * share, 0), (share, cols))

    def piece(step, own):
        return move(f"piece{step}", own, "tensor", [(i, i ^ step) for i in range(n)])

    def turned(name, own, pairs):
        return jnp.concatenate([own, move(name, own, copies, pairs)], axis=0)

    def more(bit, parts):
        return parts + [swap(f"table{bit}_{i}", part, "dp", nd, bit) for i, part in enumerate(parts)]

    def ranks(table):
        return rank_partials(ids, owner, counts, hidden, query_gradient, table, **sizes)

    def rank_sum(bit, both):
        got = swap(f"rank_sum{bit}", both, "tensor", n, bit)
        return (both.astype(F32) + got.astype(F32)).astype(BF)

    def grads(both):
        return member_grads(ids, owner, hidden, query_gradient, both, nd * owned, **sizes)

    def grad_sum(send, keep):
        for bit in reversed(bits):
            total = keep.astype(F32) + swap(f"grads{bit}", send, "dp", nd, bit).astype(F32)
            if bit != bits[0]:
                rest = total.shape[0] // 2
                keep, send = total[:rest], total[rest:].astype(BF)
        return jnp.swapaxes(total[:, :, :width], 1, 2), total[:, :, width:]

    def local():
        return local_products(ids, query_gradient, weight, width)

    def folded(acc, xs, ws, tile, first, **more):
        return fold(ids, owner, counts, acc, xs, ws, tile, first, **sizes, **more)

    table = [jnp.concatenate([jnp.swapaxes(down, 1, 2), up], axis=2)]
    if fast:
        by_one = move("outer", query_gradient, "tensor", outer)
        across = move("inner", query_gradient, "tensor", inner)
        table = more(bits[0], table)
        cuts = [cut(z ^ d) for d in (1, 2, 3)]
        acc = local()
        by_one, across, cuts, table, acc = together(by_one, across, cuts, table, acc)

        piece1, piece3 = piece(1, cuts[0]), piece(3, cuts[2])
        table = more(bits[1], table)
        both = ranks(table)
        shares = [move(f"ranks{d}", both, "tensor", [(i, i ^ d) for i in range(n)]) for d in (1, 2, 3)]
        both = sum((a.astype(F32) for a in shares), both.astype(F32)).astype(BF)
        by_one, across, piece1, piece3, both = together(by_one, across, piece1, piece3, both)

        end_two = move("inner_out", across, "tensor", outward)
        by_two = move("outer_in", by_one, "tensor", inner)
        wide1 = turned("turn_a1", piece1, turn_a)
        wide3 = turned("turn_a3", piece3, turn_a)
        send, keep = grads(both)
        end_two, by_two, wide1, wide3, send, cut2 = together(end_two, by_two, wide1, wide3, send, cuts[1])

        piece2 = piece(2, cut2)
        end_upper = move("outer_in_out0", by_two[:half], "tensor", outward)
        wide1 = [wide1, move("turn_b1", wide1, copies, turn_b)]
        wide3 = [wide3, move("turn_b3", wide3, copies, turn_b)]
        two = jnp.where(middle, by_two, end_two)
        piece2, end_upper, wide1, wide3, by_two, two, send = together(
            piece2, end_upper, wide1, wide3, by_two, two, send
        )

        wide2 = turned("turn_a2", piece2, turn_a)
        other1 = [move(f"turn_c1{i}", part, copies, turn_c) for i, part in enumerate(wide1)]
        got = swap("grads0", send, "dp", nd, bits[1])
        wide2, other1, got = together(wide2, other1, got)

        rest = got.shape[0] // 2
        total = keep.astype(F32) + got.astype(F32)
        send = total[rest:].astype(BF)
        end_lower = move("outer_in_out1", by_two[half:], "tensor", outward)
        wide2 = [wide2, move("turn_b2", wide2, copies, turn_b)]
        other3 = [move(f"turn_c3{i}", part, copies, turn_c) for i, part in enumerate(wide3)]
        acc = folded(acc, [by_one], [wide1 + other1], relative_tile, 0, table=table, both=both)
        wide2, acc, end_lower, other3, send = together(wide2, acc, end_lower, other3, send)

        got = swap("grads1", send, "dp", nd, bits[0])
        other2 = [move(f"turn_c2{i}", part, copies, turn_c) for i, part in enumerate(wide2)]
        three = jnp.where(middle, across, jnp.concatenate([end_upper, end_lower], axis=0))
        result = folded(acc, [two, three], [wide2, wide3], relative_tile, 0, final=True)
        result = folded(acc, [two, three], [other2, other3], relative_tile, 2, before=result, final=True)
        got = together(got, result)[0]
        total = total[:rest] + got.astype(F32)
        grad_down, grad_up = jnp.swapaxes(total[:, :, :width], 1, 2), total[:, :, width:]
    else:
        xs = line(query_gradient, n, z)
        wides = []
        for step in range(1, n):
            own = move(f"piece{step}", cut(lax.rem(z + step, n)), "tensor", [(i, (i + step) % n) for i in range(n)])
            wides.append((lax.all_gather(own, copies, axis=0, tiled=True),))
        for bit in bits:
            table = [jnp.concatenate(more(bit, table), axis=0)]
        both = ranks(table)
        for bit in range(n.bit_length() - 1):
            both = rank_sum(bit, both)
        grad_down, grad_up = grad_sum(*grads(both))
        acc = folded(local(), xs[:1], wides[:1], plain_tile, 0, table=table, both=both)
        result = folded(acc, xs[1:], wides[1:], plain_tile, 0, final=True)
    return result, grad_down, grad_up


def solution(mesh):
    return jax.shard_map(
        body,
        mesh=mesh,
        in_specs=(
            P(("groups", "dp"), "tensor"),
            P(("groups", "dp"), "tensor"),
            P(None, "tensor"),
            P(("groups", "dp"), "tensor", None),
            P(("groups", "dp"), None, "tensor"),
            P("groups"),
            P("groups"),
        ),
        out_specs=(
            P(("groups", "dp"), "tensor"),
            P(("groups", "dp"), "tensor", None),
            P(("groups", "dp"), None, "tensor"),
        ),
        check_vma=False,
    )
```

```python
import functools

import jax
import jax.numpy as jnp
from jax import lax
from jax.experimental import pallas as pl
from jax.experimental.pallas import tpu as pltpu
from jax.sharding import PartitionSpec as P

BLK = 128
PIECE = 256
TILE = 2 * PIECE
BF = jnp.bfloat16
F32 = jnp.float32


CHEAP = pl.CostEstimate(flops=1, bytes_accessed=1, transcendentals=0)


def move(name, a, axis, pairs):
    with jax.named_scope(name):
        return lax.ppermute(a, axis, pairs)


def swap(name, a, axis, size, bit):
    return move(name, a, axis, [(i, i ^ (1 << bit)) for i in range(size)])


def together(*values):
    return lax.optimization_barrier(values)


def contract_last(a, b):
    return lax.dot_general(a, b, (((1,), (1,)), ((), ())), preferred_element_type=F32)


def contract_first(a, b):
    return lax.dot_general(a, b, (((0,), (0,)), ((), ())), preferred_element_type=F32)


def params(mib):
    return pltpu.CompilerParams(vmem_limit_bytes=mib * 2**20)


def slot_of(block, ids, owner, *, blocks, owned, bits):
    member = owner[ids[1] * blocks + block]
    relative = (member // owned) ^ ids[1]
    slot = member % owned
    for j, bit in enumerate(bits):
        slot = slot + ((relative >> bit) & 1) * (owned << j)
    return slot


def live_count(block, ids, owner, counts, *, blocks):
    at = ids[1] * blocks + block
    last = owner.shape[0] - 1
    member = owner[at]
    closing = jnp.logical_or(at == last, owner[jnp.minimum(at + 1, last)] != member)
    return jnp.where(closing, counts[member], BLK)


def rank_kernel(ids, owner, counts, hid, cot, *refs, width, blocks, slot, held):
    b = pl.program_id(0)
    count = live_count(b, ids, owner, counts, blocks=blocks)
    parts, out = refs[:-1], refs[-1]
    for i, part in enumerate(parts):

        @pl.when(slot(b, ids, owner) // held == i)
        def _(part=part):
            act = contract_last(hid[...], part[0, :, :width])
            grad = contract_last(cot[...], part[0, :, width:])
            both = jnp.concatenate([act, grad], axis=1)
            rows = lax.broadcasted_iota(jnp.int32, both.shape, 0)
            out[...] = jnp.where(rows < count, both, 0.0).astype(BF)


def rank_partials(ids, owner, counts, hidden, cotan, table, *, blocks, owned, bits):
    width, cols = hidden.shape[1], cotan.shape[1]
    held, rank = table[0].shape[:2]
    slot = functools.partial(slot_of, blocks=blocks, owned=owned, bits=bits)

    def chosen(i):
        def index(b, ids, owner, counts):
            at = slot(b, ids, owner)
            return (jnp.where(at // held == i, at % held, 0), 0, 0)

        return pl.BlockSpec((1, rank, width + cols), index)

    return pl.pallas_call(
        functools.partial(rank_kernel, width=width, blocks=blocks, slot=slot, held=held),
        grid_spec=pltpu.PrefetchScalarGridSpec(
            num_scalar_prefetch=3,
            grid=(blocks,),
            in_specs=[
                pl.BlockSpec((BLK, width), lambda b, *s: (b, 0)),
                pl.BlockSpec((BLK, cols), lambda b, *s: (b, 0)),
            ]
            + [chosen(i) for i in range(len(table))],
            out_specs=pl.BlockSpec((BLK, 2 * rank), lambda b, *s: (b, 0)),
        ),
        out_shape=jax.ShapeDtypeStruct((blocks * BLK, 2 * rank), BF),
        compiler_params=params(16),
        cost_estimate=CHEAP,
        name="rank_partials",
    )(ids, owner, counts, hidden, cotan, *table)


def grads_kernel(ids, owner, hid, cot, both, *refs, width, blocks, slot, half):
    sends, keep, acc = refs[:half], refs[half], refs[half + 1]
    step = pl.program_id(0)
    position = jnp.where(step < half, step + half, step - half)
    rank = both.shape[1] // 2
    acc[...] = jnp.zeros_like(acc)
    for b in range(blocks):

        @pl.when(slot(b, ids, owner) == position)
        def _(b=b):
            at = pl.ds(b * BLK, BLK)
            pair = both[at, :].astype(F32)
            acc[:, :width] += contract_first(pair[:, rank:].astype(BF), hid[at, :])
            acc[:, width:] += contract_first(pair[:, :rank].astype(BF), cot[at, :])

    for i, send in enumerate(sends):

        @pl.when(step == i)
        def _(send=send):
            send[0] = acc[...].astype(BF)

    @pl.when(step >= half)
    def _():
        keep[0] = acc[...].astype(BF)


def member_grads(ids, owner, hidden, cotan, both, members, *, blocks, owned, bits):
    tokens, width = hidden.shape
    cols = cotan.shape[1]
    rank = both.shape[1] // 2
    half = members // 2
    slot = functools.partial(slot_of, blocks=blocks, owned=owned, bits=bits)
    shape = lambda count: jax.ShapeDtypeStruct((count, rank, width + cols), BF)
    *sends, keep = pl.pallas_call(
        functools.partial(
            grads_kernel, width=width, blocks=blocks, slot=slot, half=half
        ),
        grid_spec=pltpu.PrefetchScalarGridSpec(
            num_scalar_prefetch=2,
            grid=(members,),
            in_specs=[
                pl.BlockSpec((tokens, width), lambda p, *s: (0, 0)),
                pl.BlockSpec((tokens, cols), lambda p, *s: (0, 0)),
                pl.BlockSpec((tokens, 2 * rank), lambda p, *s: (0, 0)),
            ],
            out_specs=[pl.BlockSpec((1, rank, width + cols), lambda p, *s: (0, 0, 0)) for _ in range(half)]
            + [pl.BlockSpec((1, rank, width + cols), lambda p, *s: (jnp.maximum(p - half, 0), 0, 0))],
            scratch_shapes=[pltpu.VMEM((rank, width + cols), F32)],
        ),
        out_shape=[shape(1)] * half + [shape(half)],
        compiler_params=params(16),
        cost_estimate=CHEAP,
        name="member_grads",
    )(ids, owner, hidden, cotan, both)
    return sends, keep


def relative_tile(p, ids):
    core = (ids[1] & 1) ^ (p >> 1)
    x, y = ids[0], (ids[1] >> 1) & 1
    at = jnp.where(core == 0, y ^ (p & 1), 2 + (x ^ (p & 1)))
    return at, jnp.where(core == 0, x, y)


def plain_tile(p, ids):
    return p, 0


def tile_part(half, flip):
    return pl.ds(pl.multiple_of((half ^ flip) * PIECE, PIECE), PIECE)


def by_part(p, parts, run):
    if parts == 1:
        run(0)
        return
    for i in range(parts):
        pl.when(p == i)(functools.partial(run, i))


def local_kernel(ids, cot, weight, out):
    out[...] = contract_last(cot[...], weight[...])


def local_products(ids, cotan, weight, width):
    tokens, cols = cotan.shape
    tiles = width // TILE
    return pl.pallas_call(
        local_kernel,
        grid_spec=pltpu.PrefetchScalarGridSpec(
            num_scalar_prefetch=1,
            grid=(tiles,),
            in_specs=[
                pl.BlockSpec((tokens, cols), lambda p, *s: (0, 0)),
                pl.BlockSpec((TILE, cols), lambda p, i: (i[2] * tiles + p, 0)),
            ],
            out_specs=pl.BlockSpec((tokens, TILE), lambda p, *s: (0, p)),
        ),
        out_shape=jax.ShapeDtypeStruct((tokens, width), F32),
        compiler_params=params(16),
        cost_estimate=CHEAP,
        name="local_products",
    )(ids, cotan, weight)


def fold_kernel(ids, owner, counts, acc, *refs, terms, parts, tile, first, blocks, slot, table_parts, held, final):
    p = pl.program_id(0)
    xs, refs = refs[:terms], refs[terms:]
    ws, refs = refs[: terms * parts], refs[terms * parts :]
    table, out = refs[:table_parts], refs[-1]
    _, flip = tile(first + p, ids)
    rows = lax.broadcasted_iota(jnp.int32, (BLK, PIECE), 0)

    def run(i):
        total = contract_last(xs[0][...], ws[i][...])
        for t in range(1, terms):
            total += contract_last(xs[t][...], ws[t * parts + i][...])
        for half in range(2):
            to = tile_part(half, flip)
            part = acc[:, to] + total[:, half * PIECE : (half + 1) * PIECE]
            if not final:
                out[:, to] = part
                continue
            for b in range(blocks):
                at = slice(b * BLK, (b + 1) * BLK)
                count = live_count(b, ids, owner, counts, blocks=blocks)
                out[at, to] = jnp.where(rows < count, part[at], 0.0).astype(BF)

    by_part(p, parts, run)
    if table:
        both = refs[table_parts]
        rank = both.shape[1] // 2
        for b in range(blocks):
            at = slice(b * BLK, (b + 1) * BLK)
            place = slot(b, ids, owner)
            for i, part in enumerate(table):

                @pl.when(place // held == i)
                def _(at=at, place=place, part=part):
                    out[at, :] += lax.dot_general(
                        both[at, rank:],
                        part[place % held],
                        (((1,), (0,)), ((), ())),
                        preferred_element_type=F32,
                    )


def fold(ids, owner, counts, acc, xs, ws, tile, first, *, blocks, owned, bits, before=None, final=False, table=(), both=None):
    tokens, width = acc.shape
    cols = xs[0].shape[1]
    parts = len(ws[0])
    flat = [part for w in ws for part in w]
    tiles = parts if parts > 1 else flat[0].shape[0] // TILE
    slot = functools.partial(slot_of, blocks=blocks, owned=owned, bits=bits)
    block = pl.BlockSpec((tokens, TILE), lambda p, i, *s: (0, tile(first + p, i)[0]))
    operands = [ids, owner, counts, acc, *xs, *flat, *table]
    in_specs = [block]
    in_specs += [pl.BlockSpec((tokens, cols), lambda p, *s: (0, 0)) for _ in xs]
    in_specs += [pl.BlockSpec((TILE, cols), lambda p, *s: (p if parts == 1 else 0, 0)) for _ in flat]
    held = 0
    if table:
        held, rank = table[0].shape[:2]
        in_specs += [
            pl.BlockSpec((held, rank, TILE), lambda p, i, *s: (0, 0, tile(first + p, i)[0])) for _ in table
        ]
        operands.append(both)
        in_specs.append(pl.BlockSpec((tokens, 2 * rank), lambda p, *s: (0, 0)))
    alias = {} if final else {3: 0}
    if before is not None:
        alias = {len(operands): 0}
        operands.append(before)
        in_specs.append(pl.BlockSpec(memory_space=pl.ANY))
    return pl.pallas_call(
        functools.partial(
            fold_kernel,
            terms=len(xs),
            parts=parts,
            tile=tile,
            first=first,
            blocks=blocks,
            slot=slot,
            table_parts=len(table),
            held=held,
            final=final,
        ),
        grid_spec=pltpu.PrefetchScalarGridSpec(
            num_scalar_prefetch=3, grid=(tiles,), in_specs=in_specs, out_specs=block
        ),
        out_shape=jax.ShapeDtypeStruct((tokens, width), BF if final else F32),
        input_output_aliases=alias,
        compiler_params=params(28),
        cost_estimate=CHEAP,
        name="finish" if final else "fold",
    )(*operands)


def line(cotan, n, z):
    ups, downs = [], []
    a = b = cotan
    for r in range(1, n):
        a = lax.ppermute(a, "tensor", [(i, i + 1) for i in range(r - 1, n - 1)])
        b = lax.ppermute(b, "tensor", [(i, i - 1) for i in range(n - r, 0, -1)])
        ups.append(a)
        downs.append(b)
    return [jnp.where(z >= s, ups[s - 1], downs[n - s - 1]) for s in range(1, n)]


def body(hidden, query_gradient, weight, down, up, owner, counts):
    n = lax.axis_size("tensor")
    nd = lax.axis_size("dp")
    ng = lax.axis_size("groups")
    x, me, z = lax.axis_index("groups"), lax.axis_index("dp"), lax.axis_index("tensor")
    middle = jnp.logical_and(z > 0, z < n - 1)
    ids = jnp.stack([x, me, z, middle.astype(jnp.int32)]).astype(jnp.int32)
    tokens, width = hidden.shape
    cols = query_gradient.shape[1]
    owned = down.shape[0]
    share = width // (ng * nd)
    bits = tuple(range(nd.bit_length() - 2, -1, -1))
    sizes = dict(blocks=tokens // BLK, owned=owned, bits=bits)
    fast = (ng, nd, n, share) == (2, 4, 4, PIECE)

    if fast:
        y, core = me // 2, me % 2
        place = jnp.where(core == 0, 2 * y + x, 4 + 2 * x + y)
        turn_a = [(i, i ^ (4 if i % 2 == 0 else 2)) for i in range(8)]
        turn_b = [(i, i ^ (2 if i % 2 == 0 else 4)) for i in range(8)]
        turn_c = [(i, i ^ 1) for i in range(8)]
        outer, inner = [(0, 1), (1, 0), (2, 3), (3, 2)], [(1, 2), (2, 1)]
        outward = [(1, 0), (2, 3)]
    else:
        place = x * nd + me
    copies = ("groups", "dp")

    def cut(to):
        return lax.dynamic_slice(weight, (to * width + place * share, 0), (share, cols))

    def piece(step, own):
        return move(f"piece{step}", own, "tensor", [(i, i ^ step) for i in range(n)])

    def turned(name, own, pairs):
        return jnp.concatenate([own, move(name, own, copies, pairs)], axis=0)

    def more(bit, parts):
        return parts + [swap(f"table{bit}_{i}", part, "dp", nd, bit) for i, part in enumerate(parts)]

    def ranks(table):
        return rank_partials(ids, owner, counts, hidden, query_gradient, table, **sizes)

    def rank_sum(bit, both):
        got = swap(f"rank_sum{bit}", both, "tensor", n, bit)
        return (both.astype(F32) + got.astype(F32)).astype(BF)

    def grads(both):
        return member_grads(ids, owner, hidden, query_gradient, both, nd * owned, **sizes)

    def grad_sum(sends, keep):
        send = jnp.concatenate(sends, axis=0)
        for bit in reversed(bits):
            total = keep.astype(F32) + swap(f"grads{bit}", send, "dp", nd, bit).astype(F32)
            if bit != bits[0]:
                rest = total.shape[0] // 2
                keep, send = total[:rest], total[rest:].astype(BF)
        return jnp.swapaxes(total[:, :, :width], 1, 2), total[:, :, width:]

    def local():
        return local_products(ids, query_gradient, weight, width)

    def folded(acc, xs, ws, tile, first, **more):
        return fold(ids, owner, counts, acc, xs, ws, tile, first, **sizes, **more)

    table = [jnp.concatenate([jnp.swapaxes(down, 1, 2), up], axis=2)]
    if fast:
        cuts = [cut(z ^ d) for d in (1, 2, 3)]
        piece1, piece3 = piece(1, cuts[0]), piece(3, cuts[2])
        table = more(bits[0], table)
        acc = local()
        piece1, piece3, cut2, table, acc = together(piece1, piece3, cuts[1], table, acc)

        by_one = move("outer", query_gradient, "tensor", outer)
        across = move("inner", query_gradient, "tensor", inner)
        wide1 = turned("turn_a1", piece1, turn_a)
        wide3 = turned("turn_a3", piece3, turn_a)
        table = more(bits[1], table)
        both = ranks(table)
        shares = [move(f"ranks{d}", both, "tensor", [(i, i ^ d) for i in range(n)]) for d in (1, 2, 3)]
        both = sum((a.astype(F32) for a in shares), both.astype(F32)).astype(BF)
        by_one, across, wide1, wide3, both, cut2 = together(by_one, across, wide1, wide3, both, cut2)

        piece2 = piece(2, cut2)
        wide1 = [wide1, move("turn_b1", wide1, copies, turn_b)]
        wide3 = [wide3, move("turn_b3", wide3, copies, turn_b)]
        sends, keep = grads(both)
        rest = len(sends) // 2
        got = [swap(f"grads0_{i}", one, "dp", nd, bits[1]) for i, one in enumerate(sends)]
        by_one, across, piece2, wide1, wide3, far = together(by_one, across, piece2, wide1, wide3, got[rest:])

        end_two = move("inner_out", across, "tensor", outward)
        by_two = move("outer_in", by_one, "tensor", inner)
        wide2 = turned("turn_a2", piece2, turn_a)
        far = keep[rest:].astype(F32) + jnp.concatenate(far, axis=0).astype(F32)
        far = swap("grads1", far.astype(BF), "dp", nd, bits[0])
        end_two, by_two, wide2, far = together(end_two, by_two, wide2, far)

        end_three = move("outer_in_out", by_two, "tensor", outward)
        wide2 = [wide2, move("turn_b2", wide2, copies, turn_b)]
        other1 = [move(f"turn_c1{i}", part, copies, turn_c) for i, part in enumerate(wide1)]
        acc = folded(acc, [by_one], [wide1 + other1], relative_tile, 0, table=table, both=both)
        two = jnp.where(middle, by_two, end_two)
        total = keep[:rest].astype(F32) + jnp.concatenate(got[:rest], axis=0).astype(F32) + far.astype(F32)
        grad_down, grad_up = jnp.swapaxes(total[:, :, :width], 1, 2), total[:, :, width:]
        wide2, acc, end_three, two, grad_down, grad_up = together(
            wide2, acc, end_three, two, grad_down, grad_up
        )

        other2 = [move(f"turn_c2{i}", part, copies, turn_c) for i, part in enumerate(wide2)]
        other3 = [move(f"turn_c3{i}", part, copies, turn_c) for i, part in enumerate(wide3)]
        three = jnp.where(middle, across, end_three)
        result = folded(acc, [two, three], [wide2, wide3], relative_tile, 0, final=True)
        result = folded(acc, [two, three], [other2, other3], relative_tile, 2, before=result, final=True)
    else:
        xs = line(query_gradient, n, z)
        wides = []
        for step in range(1, n):
            own = move(f"piece{step}", cut(lax.rem(z + step, n)), "tensor", [(i, (i + step) % n) for i in range(n)])
            wides.append((lax.all_gather(own, copies, axis=0, tiled=True),))
        for bit in bits:
            table = [jnp.concatenate(more(bit, table), axis=0)]
        both = ranks(table)
        for bit in range(n.bit_length() - 1):
            both = rank_sum(bit, both)
        grad_down, grad_up = grad_sum(*grads(both))
        acc = folded(local(), xs[:1], wides[:1], plain_tile, 0, table=table, both=both)
        result = folded(acc, xs[1:], wides[1:], plain_tile, 0, final=True)
    return result, grad_down, grad_up


def solution(mesh):
    return jax.shard_map(
        body,
        mesh=mesh,
        in_specs=(
            P(("groups", "dp"), "tensor"),
            P(("groups", "dp"), "tensor"),
            P(None, "tensor"),
            P(("groups", "dp"), "tensor", None),
            P(("groups", "dp"), None, "tensor"),
            P("groups"),
            P("groups"),
        ),
        out_specs=(
            P(("groups", "dp"), "tensor"),
            P(("groups", "dp"), "tensor", None),
            P(("groups", "dp"), None, "tensor"),
        ),
        check_vma=False,
    )
```

```python
import functools

import jax
import jax.numpy as jnp
from jax import lax
from jax.experimental import pallas as pl
from jax.experimental.pallas import tpu as pltpu
from jax.sharding import PartitionSpec as P

BLK = 128
PIECE = 256
TILE = 2 * PIECE
BF = jnp.bfloat16
F32 = jnp.float32


CHEAP = pl.CostEstimate(flops=1, bytes_accessed=1, transcendentals=0)


def move(name, a, axis, pairs):
    with jax.named_scope(name):
        return lax.ppermute(a, axis, pairs)


def swap(name, a, axis, size, bit):
    return move(name, a, axis, [(i, i ^ (1 << bit)) for i in range(size)])


def together(*values):
    return lax.optimization_barrier(values)


def contract_last(a, b):
    return lax.dot_general(a, b, (((1,), (1,)), ((), ())), preferred_element_type=F32)


def contract_first(a, b):
    return lax.dot_general(a, b, (((0,), (0,)), ((), ())), preferred_element_type=F32)


def params(mib):
    return pltpu.CompilerParams(vmem_limit_bytes=mib * 2**20)


def slot_of(block, ids, owner, *, blocks, owned, bits):
    member = owner[ids[1] * blocks + block]
    relative = (member // owned) ^ ids[1]
    slot = member % owned
    for j, bit in enumerate(bits):
        slot = slot + ((relative >> bit) & 1) * (owned << j)
    return slot


def live_count(block, ids, owner, counts, *, blocks):
    at = ids[1] * blocks + block
    last = owner.shape[0] - 1
    member = owner[at]
    closing = jnp.logical_or(at == last, owner[jnp.minimum(at + 1, last)] != member)
    return jnp.where(closing, counts[member], BLK)


def rank_kernel(ids, owner, counts, hid, cot, *refs, blocks, slot, held):
    b = pl.program_id(0)
    count = live_count(b, ids, owner, counts, blocks=blocks)
    parts, out = refs[:-1], refs[-1]
    for i in range(len(parts) // 2):

        @pl.when(slot(b, ids, owner) // held == i)
        def _(down=parts[2 * i], up=parts[2 * i + 1]):
            act = contract_last(hid[...], down[0])
            grad = contract_last(cot[...], up[0])
            both = jnp.concatenate([act, grad], axis=1)
            rows = lax.broadcasted_iota(jnp.int32, both.shape, 0)
            out[...] = jnp.where(rows < count, both, 0.0).astype(BF)


def rank_partials(ids, owner, counts, hidden, cotan, table, *, blocks, owned, bits):
    width, cols = hidden.shape[1], cotan.shape[1]
    held, rank = table[0][0].shape[:2]
    slot = functools.partial(slot_of, blocks=blocks, owned=owned, bits=bits)

    def chosen(i, size):
        def index(b, ids, owner, counts):
            at = slot(b, ids, owner)
            return (jnp.where(at // held == i, at % held, 0), 0, 0)

        return pl.BlockSpec((1, rank, size), index)

    return pl.pallas_call(
        functools.partial(rank_kernel, blocks=blocks, slot=slot, held=held),
        grid_spec=pltpu.PrefetchScalarGridSpec(
            num_scalar_prefetch=3,
            grid=(blocks,),
            in_specs=[
                pl.BlockSpec((BLK, width), lambda b, *s: (b, 0)),
                pl.BlockSpec((BLK, cols), lambda b, *s: (b, 0)),
            ]
            + [chosen(i, size) for i in range(len(table)) for size in (width, cols)],
            out_specs=pl.BlockSpec((BLK, 2 * rank), lambda b, *s: (b, 0)),
        ),
        out_shape=jax.ShapeDtypeStruct((blocks * BLK, 2 * rank), BF),
        compiler_params=params(16),
        cost_estimate=CHEAP,
        name="rank_partials",
    )(ids, owner, counts, hidden, cotan, *[one for pair in table for one in pair])


def grads_kernel(ids, owner, hid, cot, both, *refs, width, blocks, slot, half):
    sends, keep, acc = refs[:half], refs[half], refs[half + 1]
    step = pl.program_id(0)
    position = jnp.where(step < half, step + half, step - half)
    rank = both.shape[1] // 2
    acc[...] = jnp.zeros_like(acc)
    for b in range(blocks):

        @pl.when(slot(b, ids, owner) == position)
        def _(b=b):
            at = pl.ds(b * BLK, BLK)
            pair = both[at, :].astype(F32)
            acc[:, :width] += contract_first(pair[:, rank:].astype(BF), hid[at, :])
            acc[:, width:] += contract_first(pair[:, :rank].astype(BF), cot[at, :])

    for i, send in enumerate(sends):

        @pl.when(step == i)
        def _(send=send):
            send[0] = acc[...].astype(BF)

    @pl.when(step >= half)
    def _():
        keep[0] = acc[...].astype(BF)


def member_grads(ids, owner, hidden, cotan, both, members, *, blocks, owned, bits):
    tokens, width = hidden.shape
    cols = cotan.shape[1]
    rank = both.shape[1] // 2
    half = members // 2
    slot = functools.partial(slot_of, blocks=blocks, owned=owned, bits=bits)
    shape = lambda count: jax.ShapeDtypeStruct((count, rank, width + cols), BF)
    *sends, keep = pl.pallas_call(
        functools.partial(
            grads_kernel, width=width, blocks=blocks, slot=slot, half=half
        ),
        grid_spec=pltpu.PrefetchScalarGridSpec(
            num_scalar_prefetch=2,
            grid=(members,),
            in_specs=[
                pl.BlockSpec((tokens, width), lambda p, *s: (0, 0)),
                pl.BlockSpec((tokens, cols), lambda p, *s: (0, 0)),
                pl.BlockSpec((tokens, 2 * rank), lambda p, *s: (0, 0)),
            ],
            out_specs=[pl.BlockSpec((1, rank, width + cols), lambda p, *s: (0, 0, 0)) for _ in range(half)]
            + [pl.BlockSpec((1, rank, width + cols), lambda p, *s: (jnp.maximum(p - half, 0), 0, 0))],
            scratch_shapes=[pltpu.VMEM((rank, width + cols), F32)],
        ),
        out_shape=[shape(1)] * half + [shape(half)],
        compiler_params=params(16),
        cost_estimate=CHEAP,
        name="member_grads",
    )(ids, owner, hidden, cotan, both)
    return sends, keep


def relative_tile(p, ids):
    core = (ids[1] & 1) ^ (p >> 1)
    x, y = ids[0], (ids[1] >> 1) & 1
    at = jnp.where(core == 0, y ^ (p & 1), 2 + (x ^ (p & 1)))
    return at, jnp.where(core == 0, x, y)


def plain_tile(p, ids):
    return p, 0


def tile_part(half, flip):
    return pl.ds(pl.multiple_of((half ^ flip) * PIECE, PIECE), PIECE)


def by_part(p, parts, run):
    if parts == 1:
        run(0)
        return
    for i in range(parts):
        pl.when(p == i)(functools.partial(run, i))


def local_kernel(ids, cot, weight, out):
    out[...] = contract_last(cot[...], weight[...])


def local_products(ids, cotan, weight, width):
    tokens, cols = cotan.shape
    tiles = width // TILE
    return pl.pallas_call(
        local_kernel,
        grid_spec=pltpu.PrefetchScalarGridSpec(
            num_scalar_prefetch=1,
            grid=(tiles,),
            in_specs=[
                pl.BlockSpec((tokens, cols), lambda p, *s: (0, 0)),
                pl.BlockSpec((TILE, cols), lambda p, i: (i[2] * tiles + p, 0)),
            ],
            out_specs=pl.BlockSpec((tokens, TILE), lambda p, *s: (0, p)),
        ),
        out_shape=jax.ShapeDtypeStruct((tokens, width), F32),
        compiler_params=params(16),
        cost_estimate=CHEAP,
        name="local_products",
    )(ids, cotan, weight)


def fold_kernel(ids, owner, counts, acc, *refs, terms, parts, tile, first, blocks, slot, table_parts, held, final):
    p = pl.program_id(0)
    xs, refs = refs[:terms], refs[terms:]
    ws, refs = refs[: terms * parts], refs[terms * parts :]
    table, out = refs[:table_parts], refs[-1]
    _, flip = tile(first + p, ids)
    rows = lax.broadcasted_iota(jnp.int32, (BLK, PIECE), 0)

    def run(i):
        total = contract_last(xs[0][...], ws[i][...])
        for t in range(1, terms):
            total += contract_last(xs[t][...], ws[t * parts + i][...])
        for half in range(2):
            to = tile_part(half, flip)
            part = acc[:, to] + total[:, half * PIECE : (half + 1) * PIECE]
            if not final:
                out[:, to] = part
                continue
            for b in range(blocks):
                at = slice(b * BLK, (b + 1) * BLK)
                count = live_count(b, ids, owner, counts, blocks=blocks)
                out[at, to] = jnp.where(rows < count, part[at], 0.0).astype(BF)

    by_part(p, parts, run)
    if table:
        both = refs[table_parts]
        rank = both.shape[1] // 2
        for b in range(blocks):
            at = slice(b * BLK, (b + 1) * BLK)
            place = slot(b, ids, owner)
            for i, part in enumerate(table):

                @pl.when(place // held == i)
                def _(at=at, place=place, part=part):
                    out[at, :] += lax.dot_general(
                        both[at, rank:],
                        part[place % held],
                        (((1,), (0,)), ((), ())),
                        preferred_element_type=F32,
                    )


def fold(ids, owner, counts, acc, xs, ws, tile, first, *, blocks, owned, bits, before=None, final=False, table=(), both=None):
    tokens, width = acc.shape
    cols = xs[0].shape[1]
    parts = len(ws[0])
    flat = [part for w in ws for part in w]
    tiles = parts if parts > 1 else flat[0].shape[0] // TILE
    slot = functools.partial(slot_of, blocks=blocks, owned=owned, bits=bits)
    block = pl.BlockSpec((tokens, TILE), lambda p, i, *s: (0, tile(first + p, i)[0]))
    operands = [ids, owner, counts, acc, *xs, *flat, *table]
    in_specs = [block]
    in_specs += [pl.BlockSpec((tokens, cols), lambda p, *s: (0, 0)) for _ in xs]
    in_specs += [pl.BlockSpec((TILE, cols), lambda p, *s: (p if parts == 1 else 0, 0)) for _ in flat]
    held = 0
    if table:
        held, rank = table[0].shape[:2]
        in_specs += [
            pl.BlockSpec((held, rank, TILE), lambda p, i, *s: (0, 0, tile(first + p, i)[0])) for _ in table
        ]
        operands.append(both)
        in_specs.append(pl.BlockSpec((tokens, 2 * rank), lambda p, *s: (0, 0)))
    alias = {} if final else {3: 0}
    if before is not None:
        alias = {len(operands): 0}
        operands.append(before)
        in_specs.append(pl.BlockSpec(memory_space=pl.ANY))
    return pl.pallas_call(
        functools.partial(
            fold_kernel,
            terms=len(xs),
            parts=parts,
            tile=tile,
            first=first,
            blocks=blocks,
            slot=slot,
            table_parts=len(table),
            held=held,
            final=final,
        ),
        grid_spec=pltpu.PrefetchScalarGridSpec(
            num_scalar_prefetch=3, grid=(tiles,), in_specs=in_specs, out_specs=block
        ),
        out_shape=jax.ShapeDtypeStruct((tokens, width), BF if final else F32),
        input_output_aliases=alias,
        compiler_params=params(28),
        cost_estimate=CHEAP,
        name="finish" if final else "fold",
    )(*operands)


def line(cotan, n, z):
    ups, downs = [], []
    a = b = cotan
    for r in range(1, n):
        a = lax.ppermute(a, "tensor", [(i, i + 1) for i in range(r - 1, n - 1)])
        b = lax.ppermute(b, "tensor", [(i, i - 1) for i in range(n - r, 0, -1)])
        ups.append(a)
        downs.append(b)
    return [jnp.where(z >= s, ups[s - 1], downs[n - s - 1]) for s in range(1, n)]


def body(hidden, query_gradient, weight, down, up, owner, counts):
    n = lax.axis_size("tensor")
    nd = lax.axis_size("dp")
    ng = lax.axis_size("groups")
    x, me, z = lax.axis_index("groups"), lax.axis_index("dp"), lax.axis_index("tensor")
    middle = jnp.logical_and(z > 0, z < n - 1)
    ids = jnp.stack([x, me, z, middle.astype(jnp.int32)]).astype(jnp.int32)
    tokens, width = hidden.shape
    cols = query_gradient.shape[1]
    owned = down.shape[0]
    share = width // (ng * nd)
    bits = tuple(range(nd.bit_length() - 2, -1, -1))
    sizes = dict(blocks=tokens // BLK, owned=owned, bits=bits)
    fast = (ng, nd, n, share) == (2, 4, 4, PIECE)

    if fast:
        y, core = me // 2, me % 2
        place = jnp.where(core == 0, 2 * y + x, 4 + 2 * x + y)
        turn_a = [(i, i ^ (4 if i % 2 == 0 else 2)) for i in range(8)]
        turn_b = [(i, i ^ (2 if i % 2 == 0 else 4)) for i in range(8)]
        turn_c = [(i, i ^ 1) for i in range(8)]
        outer, inner = [(0, 1), (1, 0), (2, 3), (3, 2)], [(1, 2), (2, 1)]
        outward = [(1, 0), (2, 3)]
    else:
        place = x * nd + me
    copies = ("groups", "dp")

    def cut(to):
        return lax.dynamic_slice(weight, (to * width + place * share, 0), (share, cols))

    def piece(step, own):
        return move(f"piece{step}", own, "tensor", [(i, i ^ step) for i in range(n)])

    def turned(name, own, pairs):
        return jnp.concatenate([own, move(name, own, copies, pairs)], axis=0)

    def more(bit, parts):
        return parts + [
            (swap(f"down{bit}_{i}", down, "dp", nd, bit), swap(f"up{bit}_{i}", up, "dp", nd, bit))
            for i, (down, up) in enumerate(parts)
        ]

    def ranks(table):
        return rank_partials(ids, owner, counts, hidden, query_gradient, table, **sizes)

    def rank_sum(bit, both):
        got = swap(f"rank_sum{bit}", both, "tensor", n, bit)
        return (both.astype(F32) + got.astype(F32)).astype(BF)

    def grads(both):
        return member_grads(ids, owner, hidden, query_gradient, both, nd * owned, **sizes)

    def grad_sum(sends, keep):
        send = jnp.concatenate(sends, axis=0)
        for bit in reversed(bits):
            total = keep.astype(F32) + swap(f"grads{bit}", send, "dp", nd, bit).astype(F32)
            if bit != bits[0]:
                rest = total.shape[0] // 2
                keep, send = total[:rest], total[rest:].astype(BF)
        return jnp.swapaxes(total[:, :, :width], 1, 2), total[:, :, width:]

    def local():
        return local_products(ids, query_gradient, weight, width)

    def folded(acc, xs, ws, tile, first, **more):
        return fold(ids, owner, counts, acc, xs, ws, tile, first, **sizes, **more)

    if fast:
        piece1, piece3 = piece(1, cut(z ^ 1)), piece(3, cut(z ^ 3))
        table = more(bits[0], [(jnp.swapaxes(down, 1, 2), up)])
        cut2 = cut(z ^ 2)
        acc = local()
        piece1, piece3, cut2, table, acc = together(piece1, piece3, cut2, table, acc)

        by_one = move("outer", query_gradient, "tensor", outer)
        across = move("inner", query_gradient, "tensor", inner)
        wide1 = turned("turn_a1", piece1, turn_a)
        wide3 = turned("turn_a3", piece3, turn_a)
        table = more(bits[1], table)
        both = ranks(table)
        both = rank_sum(1, both)
        by_one, across, wide1, wide3, both, cut2 = together(by_one, across, wide1, wide3, both, cut2)

        piece2 = piece(2, cut2)
        wide1 = [wide1, move("turn_b1", wide1, copies, turn_b)]
        wide3 = [wide3, move("turn_b3", wide3, copies, turn_b)]
        both = rank_sum(0, both)
        sends, keep = grads(both)
        rest = len(sends) // 2
        got = [swap(f"grads0_{i}", one, "dp", nd, bits[1]) for i, one in enumerate(sends)]
        by_one, across, piece2, wide1, wide3, far = together(by_one, across, piece2, wide1, wide3, got[rest:])

        end_two = move("inner_out", across, "tensor", outward)
        by_two = move("outer_in", by_one, "tensor", inner)
        wide2 = turned("turn_a2", piece2, turn_a)
        far = keep[rest:].astype(F32) + jnp.concatenate(far, axis=0).astype(F32)
        far = swap("grads1", far.astype(BF), "dp", nd, bits[0])
        end_two, by_two, wide2, far = together(end_two, by_two, wide2, far)

        end_three = move("outer_in_out", by_two, "tensor", outward)
        wide2 = [wide2, move("turn_b2", wide2, copies, turn_b)]
        other1 = [move(f"turn_c1{i}", part, copies, turn_c) for i, part in enumerate(wide1)]
        acc = folded(acc, [by_one], [wide1 + other1], relative_tile, 0, table=[pair[0] for pair in table], both=both)
        two = jnp.where(middle, by_two, end_two)
        total = keep[:rest].astype(F32) + jnp.concatenate(got[:rest], axis=0).astype(F32) + far.astype(F32)
        grad_down, grad_up = jnp.swapaxes(total[:, :, :width], 1, 2), total[:, :, width:]
        wide2, acc, end_three, two, grad_down, grad_up = together(
            wide2, acc, end_three, two, grad_down, grad_up
        )

        other2 = [move(f"turn_c2{i}", part, copies, turn_c) for i, part in enumerate(wide2)]
        other3 = [move(f"turn_c3{i}", part, copies, turn_c) for i, part in enumerate(wide3)]
        three = jnp.where(middle, across, end_three)
        result = folded(acc, [two, three], [wide2, wide3], relative_tile, 0, final=True)
        result = folded(acc, [two, three], [other2, other3], relative_tile, 2, before=result, final=True)
    else:
        table = [(jnp.swapaxes(down, 1, 2), up)]
        xs = line(query_gradient, n, z)
        wides = []
        for step in range(1, n):
            own = move(f"piece{step}", cut(lax.rem(z + step, n)), "tensor", [(i, (i + step) % n) for i in range(n)])
            wides.append((lax.all_gather(own, copies, axis=0, tiled=True),))
        for bit in bits:
            table = [tuple(jnp.concatenate(pair, axis=0) for pair in zip(*more(bit, table)))]
        both = ranks(table)
        for bit in range(n.bit_length() - 1):
            both = rank_sum(bit, both)
        grad_down, grad_up = grad_sum(*grads(both))
        acc = folded(local(), xs[:1], wides[:1], plain_tile, 0, table=[pair[0] for pair in table], both=both)
        result = folded(acc, xs[1:], wides[1:], plain_tile, 0, final=True)
    return result, grad_down, grad_up


def solution(mesh):
    return jax.shard_map(
        body,
        mesh=mesh,
        in_specs=(
            P(("groups", "dp"), "tensor"),
            P(("groups", "dp"), "tensor"),
            P(None, "tensor"),
            P(("groups", "dp"), "tensor", None),
            P(("groups", "dp"), None, "tensor"),
            P("groups"),
            P("groups"),
        ),
        out_specs=(
            P(("groups", "dp"), "tensor"),
            P(("groups", "dp"), "tensor", None),
            P(("groups", "dp"), None, "tensor"),
        ),
        check_vma=False,
    )
```

```python
import functools

import jax
import jax.numpy as jnp
from jax import lax
from jax.experimental import pallas as pl
from jax.experimental.pallas import tpu as pltpu
from jax.sharding import PartitionSpec as P

BLK = 128
PIECE = 256
TILE = 2 * PIECE
BF = jnp.bfloat16
F32 = jnp.float32


CHEAP = pl.CostEstimate(flops=1, bytes_accessed=1, transcendentals=0)


def move(name, a, axis, pairs):
    with jax.named_scope(name):
        return lax.ppermute(a, axis, pairs)


def swap(name, a, axis, size, bit):
    return move(name, a, axis, [(i, i ^ (1 << bit)) for i in range(size)])


def together(*values):
    return lax.optimization_barrier(values)


def contract_last(a, b):
    return lax.dot_general(a, b, (((1,), (1,)), ((), ())), preferred_element_type=F32)


def contract_first(a, b):
    return lax.dot_general(a, b, (((0,), (0,)), ((), ())), preferred_element_type=F32)


def params(mib):
    return pltpu.CompilerParams(vmem_limit_bytes=mib * 2**20)


def slot_of(block, ids, owner, *, blocks, owned, bits):
    member = owner[ids[1] * blocks + block]
    relative = (member // owned) ^ ids[1]
    slot = member % owned
    for j, bit in enumerate(bits):
        slot = slot + ((relative >> bit) & 1) * (owned << j)
    return slot


def live_count(block, ids, owner, counts, *, blocks):
    at = ids[1] * blocks + block
    last = owner.shape[0] - 1
    member = owner[at]
    closing = jnp.logical_or(at == last, owner[jnp.minimum(at + 1, last)] != member)
    return jnp.where(closing, counts[member], BLK)


def rank_kernel(ids, owner, counts, hid, cot, *refs, blocks, slot, held):
    b = pl.program_id(0)
    count = live_count(b, ids, owner, counts, blocks=blocks)
    parts, out = refs[:-1], refs[-1]
    for i in range(len(parts) // 2):

        @pl.when(slot(b, ids, owner) // held == i)
        def _(down=parts[2 * i], up=parts[2 * i + 1]):
            act = contract_last(hid[...], down[0])
            grad = contract_last(cot[...], up[0])
            both = jnp.concatenate([act, grad], axis=1)
            rows = lax.broadcasted_iota(jnp.int32, both.shape, 0)
            out[...] = jnp.where(rows < count, both, 0.0).astype(BF)


def rank_partials(ids, owner, counts, hidden, cotan, table, *, blocks, owned, bits):
    width, cols = hidden.shape[1], cotan.shape[1]
    held, rank = table[0][0].shape[:2]
    slot = functools.partial(slot_of, blocks=blocks, owned=owned, bits=bits)

    def chosen(i, size):
        def index(b, ids, owner, counts):
            at = slot(b, ids, owner)
            return (jnp.where(at // held == i, at % held, 0), 0, 0)

        return pl.BlockSpec((1, rank, size), index)

    return pl.pallas_call(
        functools.partial(rank_kernel, blocks=blocks, slot=slot, held=held),
        grid_spec=pltpu.PrefetchScalarGridSpec(
            num_scalar_prefetch=3,
            grid=(blocks,),
            in_specs=[
                pl.BlockSpec((BLK, width), lambda b, *s: (b, 0)),
                pl.BlockSpec((BLK, cols), lambda b, *s: (b, 0)),
            ]
            + [chosen(i, size) for i in range(len(table)) for size in (width, cols)],
            out_specs=pl.BlockSpec((BLK, 2 * rank), lambda b, *s: (b, 0)),
        ),
        out_shape=jax.ShapeDtypeStruct((blocks * BLK, 2 * rank), BF),
        compiler_params=params(16),
        cost_estimate=CHEAP,
        name="rank_partials",
    )(ids, owner, counts, hidden, cotan, *[one for pair in table for one in pair])


def grads_kernel(ids, owner, hid, cot, both, *refs, width, blocks, slot, half):
    sends, keep, acc = refs[:half], refs[half], refs[half + 1]
    step = pl.program_id(0)
    position = jnp.where(step < half, step + half, step - half)
    rank = both.shape[1] // 2
    acc[...] = jnp.zeros_like(acc)
    for b in range(blocks):

        @pl.when(slot(b, ids, owner) == position)
        def _(b=b):
            at = pl.ds(b * BLK, BLK)
            pair = both[at, :].astype(F32)
            acc[:, :width] += contract_first(pair[:, rank:].astype(BF), hid[at, :])
            acc[:, width:] += contract_first(pair[:, :rank].astype(BF), cot[at, :])

    for i, send in enumerate(sends):

        @pl.when(step == i)
        def _(send=send):
            send[0] = acc[...].astype(BF)

    @pl.when(step >= half)
    def _():
        keep[0] = acc[...].astype(BF)


def member_grads(ids, owner, hidden, cotan, both, members, *, blocks, owned, bits):
    tokens, width = hidden.shape
    cols = cotan.shape[1]
    rank = both.shape[1] // 2
    half = members // 2
    slot = functools.partial(slot_of, blocks=blocks, owned=owned, bits=bits)
    shape = lambda count: jax.ShapeDtypeStruct((count, rank, width + cols), BF)
    *sends, keep = pl.pallas_call(
        functools.partial(
            grads_kernel, width=width, blocks=blocks, slot=slot, half=half
        ),
        grid_spec=pltpu.PrefetchScalarGridSpec(
            num_scalar_prefetch=2,
            grid=(members,),
            in_specs=[
                pl.BlockSpec((tokens, width), lambda p, *s: (0, 0)),
                pl.BlockSpec((tokens, cols), lambda p, *s: (0, 0)),
                pl.BlockSpec((tokens, 2 * rank), lambda p, *s: (0, 0)),
            ],
            out_specs=[pl.BlockSpec((1, rank, width + cols), lambda p, *s: (0, 0, 0)) for _ in range(half)]
            + [pl.BlockSpec((1, rank, width + cols), lambda p, *s: (jnp.maximum(p - half, 0), 0, 0))],
            scratch_shapes=[pltpu.VMEM((rank, width + cols), F32)],
        ),
        out_shape=[shape(1)] * half + [shape(half)],
        compiler_params=params(16),
        cost_estimate=CHEAP,
        name="member_grads",
    )(ids, owner, hidden, cotan, both)
    return sends, keep


def relative_tile(p, ids):
    core = (ids[1] & 1) ^ (p >> 1)
    x, y = ids[0], (ids[1] >> 1) & 1
    at = jnp.where(core == 0, y ^ (p & 1), 2 + (x ^ (p & 1)))
    return at, jnp.where(core == 0, x, y)


def plain_tile(p, ids):
    return p, 0


def tile_part(half, flip):
    return pl.ds(pl.multiple_of((half ^ flip) * PIECE, PIECE), PIECE)


def by_part(p, parts, run):
    if parts == 1:
        run(0)
        return
    for i in range(parts):
        pl.when(p == i)(functools.partial(run, i))


def local_kernel(ids, cot, weight, out):
    out[...] = contract_last(cot[...], weight[...])


def local_products(ids, cotan, weight, width):
    tokens, cols = cotan.shape
    tiles = width // TILE
    return pl.pallas_call(
        local_kernel,
        grid_spec=pltpu.PrefetchScalarGridSpec(
            num_scalar_prefetch=1,
            grid=(tiles,),
            in_specs=[
                pl.BlockSpec((tokens, cols), lambda p, *s: (0, 0)),
                pl.BlockSpec((TILE, cols), lambda p, i: (i[2] * tiles + p, 0)),
            ],
            out_specs=pl.BlockSpec((tokens, TILE), lambda p, *s: (0, p)),
        ),
        out_shape=jax.ShapeDtypeStruct((tokens, width), F32),
        compiler_params=params(16),
        cost_estimate=CHEAP,
        name="local_products",
    )(ids, cotan, weight)


def fold_kernel(ids, owner, counts, acc, *refs, terms, parts, tile, first, blocks, slot, table_parts, held, final):
    p = pl.program_id(0)
    xs, refs = refs[:terms], refs[terms:]
    ws, refs = refs[: terms * parts], refs[terms * parts :]
    table, out = refs[:table_parts], refs[-1]
    _, flip = tile(first + p, ids)
    rows = lax.broadcasted_iota(jnp.int32, (BLK, PIECE), 0)

    def run(i):
        total = contract_last(xs[0][...], ws[i][...])
        for t in range(1, terms):
            total += contract_last(xs[t][...], ws[t * parts + i][...])
        for half in range(2):
            to = tile_part(half, flip)
            part = acc[:, to] + total[:, half * PIECE : (half + 1) * PIECE]
            if not final:
                out[:, to] = part
                continue
            for b in range(blocks):
                at = slice(b * BLK, (b + 1) * BLK)
                count = live_count(b, ids, owner, counts, blocks=blocks)
                out[at, to] = jnp.where(rows < count, part[at], 0.0).astype(BF)

    by_part(p, parts, run)
    if table:
        both = refs[table_parts]
        rank = both.shape[1] // 2
        for b in range(blocks):
            at = slice(b * BLK, (b + 1) * BLK)
            place = slot(b, ids, owner)
            for i, part in enumerate(table):

                @pl.when(place // held == i)
                def _(at=at, place=place, part=part):
                    out[at, :] += lax.dot_general(
                        both[at, rank:],
                        part[place % held],
                        (((1,), (0,)), ((), ())),
                        preferred_element_type=F32,
                    )


def fold(ids, owner, counts, acc, xs, ws, tile, first, *, blocks, owned, bits, before=None, final=False, table=(), both=None):
    tokens, width = acc.shape
    cols = xs[0].shape[1]
    parts = len(ws[0])
    flat = [part for w in ws for part in w]
    tiles = parts if parts > 1 else flat[0].shape[0] // TILE
    slot = functools.partial(slot_of, blocks=blocks, owned=owned, bits=bits)
    block = pl.BlockSpec((tokens, TILE), lambda p, i, *s: (0, tile(first + p, i)[0]))
    operands = [ids, owner, counts, acc, *xs, *flat, *table]
    in_specs = [block]
    in_specs += [pl.BlockSpec((tokens, cols), lambda p, *s: (0, 0)) for _ in xs]
    in_specs += [pl.BlockSpec((TILE, cols), lambda p, *s: (p if parts == 1 else 0, 0)) for _ in flat]
    held = 0
    if table:
        held, rank = table[0].shape[:2]
        in_specs += [
            pl.BlockSpec((held, rank, TILE), lambda p, i, *s: (0, 0, tile(first + p, i)[0])) for _ in table
        ]
        operands.append(both)
        in_specs.append(pl.BlockSpec((tokens, 2 * rank), lambda p, *s: (0, 0)))
    alias = {} if final else {3: 0}
    if before is not None:
        alias = {len(operands): 0}
        operands.append(before)
        in_specs.append(pl.BlockSpec(memory_space=pl.ANY))
    return pl.pallas_call(
        functools.partial(
            fold_kernel,
            terms=len(xs),
            parts=parts,
            tile=tile,
            first=first,
            blocks=blocks,
            slot=slot,
            table_parts=len(table),
            held=held,
            final=final,
        ),
        grid_spec=pltpu.PrefetchScalarGridSpec(
            num_scalar_prefetch=3, grid=(tiles,), in_specs=in_specs, out_specs=block
        ),
        out_shape=jax.ShapeDtypeStruct((tokens, width), BF if final else F32),
        input_output_aliases=alias,
        compiler_params=params(28),
        cost_estimate=CHEAP,
        name="finish" if final else "fold",
    )(*operands)


def line(cotan, n, z):
    ups, downs = [], []
    a = b = cotan
    for r in range(1, n):
        a = lax.ppermute(a, "tensor", [(i, i + 1) for i in range(r - 1, n - 1)])
        b = lax.ppermute(b, "tensor", [(i, i - 1) for i in range(n - r, 0, -1)])
        ups.append(a)
        downs.append(b)
    return [jnp.where(z >= s, ups[s - 1], downs[n - s - 1]) for s in range(1, n)]


def body(hidden, query_gradient, weight, down, up, owner, counts):
    n = lax.axis_size("tensor")
    nd = lax.axis_size("dp")
    ng = lax.axis_size("groups")
    x, me, z = lax.axis_index("groups"), lax.axis_index("dp"), lax.axis_index("tensor")
    middle = jnp.logical_and(z > 0, z < n - 1)
    ids = jnp.stack([x, me, z, middle.astype(jnp.int32)]).astype(jnp.int32)
    tokens, width = hidden.shape
    cols = query_gradient.shape[1]
    owned = down.shape[0]
    share = width // (ng * nd)
    bits = tuple(range(nd.bit_length() - 2, -1, -1))
    sizes = dict(blocks=tokens // BLK, owned=owned, bits=bits)
    fast = (ng, nd, n, share) == (2, 4, 4, PIECE)

    if fast:
        y, core = me // 2, me % 2
        place = jnp.where(core == 0, 2 * y + x, 4 + 2 * x + y)
        turn_a = [(i, i ^ (4 if i % 2 == 0 else 2)) for i in range(8)]
        turn_b = [(i, i ^ (2 if i % 2 == 0 else 4)) for i in range(8)]
        turn_c = [(i, i ^ 1) for i in range(8)]
        outer, inner = [(0, 1), (1, 0), (2, 3), (3, 2)], [(1, 2), (2, 1)]
        outward = [(1, 0), (2, 3)]
    else:
        place = x * nd + me
    copies = ("groups", "dp")

    def cut(to):
        return lax.dynamic_slice(weight, (to * width + place * share, 0), (share, cols))

    def piece(step, own):
        return move(f"piece{step}", own, "tensor", [(i, i ^ step) for i in range(n)])

    def turned(name, own, pairs):
        return jnp.concatenate([own, move(name, own, copies, pairs)], axis=0)

    def more(bit, parts):
        return parts + [
            (swap(f"down{bit}_{i}", down, "dp", nd, bit), swap(f"up{bit}_{i}", up, "dp", nd, bit))
            for i, (down, up) in enumerate(parts)
        ]

    def ranks(table):
        return rank_partials(ids, owner, counts, hidden, query_gradient, table, **sizes)

    def rank_sum(bit, both):
        got = swap(f"rank_sum{bit}", both, "tensor", n, bit)
        return (both.astype(F32) + got.astype(F32)).astype(BF)

    def grads(both):
        return member_grads(ids, owner, hidden, query_gradient, both, nd * owned, **sizes)

    def grad_sum(sends, keep):
        send = jnp.concatenate(sends, axis=0)
        for bit in reversed(bits):
            total = keep.astype(F32) + swap(f"grads{bit}", send, "dp", nd, bit).astype(F32)
            if bit != bits[0]:
                rest = total.shape[0] // 2
                keep, send = total[:rest], total[rest:].astype(BF)
        return jnp.swapaxes(total[:, :, :width], 1, 2), total[:, :, width:]

    def local():
        return local_products(ids, query_gradient, weight, width)

    def folded(acc, xs, ws, tile, first, **more):
        return fold(ids, owner, counts, acc, xs, ws, tile, first, **sizes, **more)

    if fast:
        piece1, piece3 = piece(1, cut(z ^ 1)), piece(3, cut(z ^ 3))
        table = more(bits[0], [(jnp.swapaxes(down, 1, 2), up)])
        cut2 = cut(z ^ 2)
        acc = local()
        piece1, piece3, cut2, table, acc = together(piece1, piece3, cut2, table, acc)

        by_one = move("outer", query_gradient, "tensor", outer)
        across = move("inner", query_gradient, "tensor", inner)
        wide1 = turned("turn_a1", piece1, turn_a)
        wide3 = turned("turn_a3", piece3, turn_a)
        table = more(bits[1], table)
        both = ranks(table)
        both = rank_sum(1, both)
        by_one, across, wide1, wide3, both, cut2 = together(by_one, across, wide1, wide3, both, cut2)

        half = tokens // 2
        one0, one1, over0, over1 = by_one[:half], by_one[half:], across[:half], across[half:]
        piece2 = piece(2, cut2)
        end_two0 = move("inner_out0", over0, "tensor", outward)
        wide1 = [wide1, move("turn_b1", wide1, copies, turn_b)]
        wide3 = [wide3, move("turn_b3", wide3, copies, turn_b)]
        both = rank_sum(0, both)
        sends, keep = grads(both)
        rest = len(sends) // 2
        one0, one1, over1, end_two0, piece2, wide1, wide3, sends = together(
            one0, one1, over1, end_two0, piece2, wide1, wide3, sends
        )

        end_two1 = move("inner_out1", over1, "tensor", outward)
        two0 = move("outer_in0", one0, "tensor", inner)
        two1 = move("outer_in1", one1, "tensor", inner)
        end_three0 = move("outer_in_out0", two0, "tensor", outward)
        wide2 = turned("turn_a2", piece2, turn_a)
        got = [swap(f"grads0_{i}", one, "dp", nd, bits[1]) for i, one in enumerate(sends)]
        far = keep[rest:].astype(F32) + jnp.concatenate(got[rest:], axis=0).astype(F32)
        far = swap("grads1", far.astype(BF), "dp", nd, bits[0])
        end_two1, two0, two1, end_three0, wide1, wide2, far = together(
            end_two1, two0, two1, end_three0, wide1, wide2, far
        )

        end_three1 = move("outer_in_out1", two1, "tensor", outward)
        wide2 = [wide2, move("turn_b2", wide2, copies, turn_b)]
        other1 = [move(f"turn_c1{i}", part, copies, turn_c) for i, part in enumerate(wide1)]
        acc = folded(acc, [by_one], [wide1 + other1], relative_tile, 0, table=[pair[0] for pair in table], both=both)
        two = jnp.where(
            middle, jnp.concatenate([two0, two1], axis=0), jnp.concatenate([end_two0, end_two1], axis=0)
        )
        total = keep[:rest].astype(F32) + jnp.concatenate(got[:rest], axis=0).astype(F32) + far.astype(F32)
        grad_down, grad_up = jnp.swapaxes(total[:, :, :width], 1, 2), total[:, :, width:]
        wide2, acc, end_three1, two, grad_down, grad_up = together(
            wide2, acc, end_three1, two, grad_down, grad_up
        )
        end_three = jnp.concatenate([end_three0, end_three1], axis=0)

        other2 = [move(f"turn_c2{i}", part, copies, turn_c) for i, part in enumerate(wide2)]
        other3 = [move(f"turn_c3{i}", part, copies, turn_c) for i, part in enumerate(wide3)]
        three = jnp.where(middle, across, end_three)
        result = folded(acc, [two, three], [wide2, wide3], relative_tile, 0, final=True)
        result = folded(acc, [two, three], [other2, other3], relative_tile, 2, before=result, final=True)
    else:
        table = [(jnp.swapaxes(down, 1, 2), up)]
        xs = line(query_gradient, n, z)
        wides = []
        for step in range(1, n):
            own = move(f"piece{step}", cut(lax.rem(z + step, n)), "tensor", [(i, (i + step) % n) for i in range(n)])
            wides.append((lax.all_gather(own, copies, axis=0, tiled=True),))
        for bit in bits:
            table = [tuple(jnp.concatenate(pair, axis=0) for pair in zip(*more(bit, table)))]
        both = ranks(table)
        for bit in range(n.bit_length() - 1):
            both = rank_sum(bit, both)
        grad_down, grad_up = grad_sum(*grads(both))
        acc = folded(local(), xs[:1], wides[:1], plain_tile, 0, table=[pair[0] for pair in table], both=both)
        result = folded(acc, xs[1:], wides[1:], plain_tile, 0, final=True)
    return result, grad_down, grad_up


def solution(mesh):
    return jax.shard_map(
        body,
        mesh=mesh,
        in_specs=(
            P(("groups", "dp"), "tensor"),
            P(("groups", "dp"), "tensor"),
            P(None, "tensor"),
            P(("groups", "dp"), "tensor", None),
            P(("groups", "dp"), None, "tensor"),
            P("groups"),
            P("groups"),
        ),
        out_specs=(
            P(("groups", "dp"), "tensor"),
            P(("groups", "dp"), "tensor", None),
            P(("groups", "dp"), None, "tensor"),
        ),
        check_vma=False,
    )
```

```python
import functools

import jax
import jax.numpy as jnp
from jax import lax
from jax.experimental import pallas as pl
from jax.experimental.pallas import tpu as pltpu
from jax.sharding import PartitionSpec as P

BLK = 128
PIECE = 256
TILE = 2 * PIECE
BF = jnp.bfloat16
F32 = jnp.float32


CHEAP = pl.CostEstimate(flops=1, bytes_accessed=1, transcendentals=0)


def move(name, a, axis, pairs):
    with jax.named_scope(name):
        return lax.ppermute(a, axis, pairs)


def swap(name, a, axis, size, bit):
    return move(name, a, axis, [(i, i ^ (1 << bit)) for i in range(size)])


def together(*values):
    return lax.optimization_barrier(values)


def contract_last(a, b):
    return lax.dot_general(a, b, (((1,), (1,)), ((), ())), preferred_element_type=F32)


def contract_first(a, b):
    return lax.dot_general(a, b, (((0,), (0,)), ((), ())), preferred_element_type=F32)


def params(mib):
    return pltpu.CompilerParams(vmem_limit_bytes=mib * 2**20)


def slot_of(block, ids, owner, *, blocks, owned, bits):
    member = owner[ids[1] * blocks + block]
    relative = (member // owned) ^ ids[1]
    slot = member % owned
    for j, bit in enumerate(bits):
        slot = slot + ((relative >> bit) & 1) * (owned << j)
    return slot


def live_count(block, ids, owner, counts, *, blocks):
    at = ids[1] * blocks + block
    last = owner.shape[0] - 1
    member = owner[at]
    closing = jnp.logical_or(at == last, owner[jnp.minimum(at + 1, last)] != member)
    return jnp.where(closing, counts[member], BLK)


def rank_kernel(ids, owner, counts, hid, cot, *refs, blocks, slot, held):
    b = pl.program_id(0)
    count = live_count(b, ids, owner, counts, blocks=blocks)
    parts, out = refs[:-1], refs[-1]
    for i in range(len(parts) // 2):

        @pl.when(slot(b, ids, owner) // held == i)
        def _(down=parts[2 * i], up=parts[2 * i + 1]):
            act = contract_last(hid[...], down[0])
            grad = contract_last(cot[...], up[0])
            both = jnp.concatenate([act, grad], axis=1)
            rows = lax.broadcasted_iota(jnp.int32, both.shape, 0)
            out[...] = jnp.where(rows < count, both, 0.0).astype(BF)


def rank_partials(ids, owner, counts, hidden, cotan, table, *, blocks, owned, bits):
    width, cols = hidden.shape[1], cotan.shape[1]
    held, rank = table[0][0].shape[:2]
    slot = functools.partial(slot_of, blocks=blocks, owned=owned, bits=bits)

    def chosen(i, size):
        def index(b, ids, owner, counts):
            at = slot(b, ids, owner)
            return (jnp.where(at // held == i, at % held, 0), 0, 0)

        return pl.BlockSpec((1, rank, size), index)

    return pl.pallas_call(
        functools.partial(rank_kernel, blocks=blocks, slot=slot, held=held),
        grid_spec=pltpu.PrefetchScalarGridSpec(
            num_scalar_prefetch=3,
            grid=(blocks,),
            in_specs=[
                pl.BlockSpec((BLK, width), lambda b, *s: (b, 0)),
                pl.BlockSpec((BLK, cols), lambda b, *s: (b, 0)),
            ]
            + [chosen(i, size) for i in range(len(table)) for size in (width, cols)],
            out_specs=pl.BlockSpec((BLK, 2 * rank), lambda b, *s: (b, 0)),
        ),
        out_shape=jax.ShapeDtypeStruct((blocks * BLK, 2 * rank), BF),
        compiler_params=params(16),
        cost_estimate=CHEAP,
        name="rank_partials",
    )(ids, owner, counts, hidden, cotan, *[one for pair in table for one in pair])


def grads_kernel(ids, owner, hid, cot, both, *refs, width, blocks, slot, half):
    sends, keep, acc = refs[:half], refs[half], refs[half + 1]
    step = pl.program_id(0)
    position = jnp.where(step < half, step + half, step - half)
    rank = both.shape[1] // 2
    acc[...] = jnp.zeros_like(acc)
    for b in range(blocks):

        @pl.when(slot(b, ids, owner) == position)
        def _(b=b):
            at = pl.ds(b * BLK, BLK)
            pair = both[at, :].astype(F32)
            acc[:, :width] += contract_first(pair[:, rank:].astype(BF), hid[at, :])
            acc[:, width:] += contract_first(pair[:, :rank].astype(BF), cot[at, :])

    for i, send in enumerate(sends):

        @pl.when(step == i)
        def _(send=send):
            send[0] = acc[...].astype(BF)

    @pl.when(step >= half)
    def _():
        keep[0] = acc[...].astype(BF)


def member_grads(ids, owner, hidden, cotan, both, members, *, blocks, owned, bits):
    tokens, width = hidden.shape
    cols = cotan.shape[1]
    rank = both.shape[1] // 2
    half = members // 2
    slot = functools.partial(slot_of, blocks=blocks, owned=owned, bits=bits)
    shape = lambda count: jax.ShapeDtypeStruct((count, rank, width + cols), BF)
    *sends, keep = pl.pallas_call(
        functools.partial(
            grads_kernel, width=width, blocks=blocks, slot=slot, half=half
        ),
        grid_spec=pltpu.PrefetchScalarGridSpec(
            num_scalar_prefetch=2,
            grid=(members,),
            in_specs=[
                pl.BlockSpec((tokens, width), lambda p, *s: (0, 0)),
                pl.BlockSpec((tokens, cols), lambda p, *s: (0, 0)),
                pl.BlockSpec((tokens, 2 * rank), lambda p, *s: (0, 0)),
            ],
            out_specs=[pl.BlockSpec((1, rank, width + cols), lambda p, *s: (0, 0, 0)) for _ in range(half)]
            + [pl.BlockSpec((1, rank, width + cols), lambda p, *s: (jnp.maximum(p - half, 0), 0, 0))],
            scratch_shapes=[pltpu.VMEM((rank, width + cols), F32)],
        ),
        out_shape=[shape(1)] * half + [shape(half)],
        compiler_params=params(16),
        cost_estimate=CHEAP,
        name="member_grads",
    )(ids, owner, hidden, cotan, both)
    return sends, keep


def relative_tile(p, ids):
    core = (ids[1] & 1) ^ (p >> 1)
    x, y = ids[0], (ids[1] >> 1) & 1
    at = jnp.where(core == 0, y ^ (p & 1), 2 + (x ^ (p & 1)))
    return at, jnp.where(core == 0, x, y)


def plain_tile(p, ids):
    return p, 0


def tile_part(half, flip):
    return pl.ds(pl.multiple_of((half ^ flip) * PIECE, PIECE), PIECE)


def by_part(p, parts, run):
    if parts == 1:
        run(0)
        return
    for i in range(parts):
        pl.when(p == i)(functools.partial(run, i))


def local_kernel(ids, cot, weight, out):
    out[...] = contract_last(cot[...], weight[...])


def local_products(ids, cotan, weight, width):
    tokens, cols = cotan.shape
    tiles = width // TILE
    return pl.pallas_call(
        local_kernel,
        grid_spec=pltpu.PrefetchScalarGridSpec(
            num_scalar_prefetch=1,
            grid=(tiles,),
            in_specs=[
                pl.BlockSpec((tokens, cols), lambda p, *s: (0, 0)),
                pl.BlockSpec((TILE, cols), lambda p, i: (i[2] * tiles + p, 0)),
            ],
            out_specs=pl.BlockSpec((tokens, TILE), lambda p, *s: (0, p)),
        ),
        out_shape=jax.ShapeDtypeStruct((tokens, width), F32),
        compiler_params=params(16),
        cost_estimate=CHEAP,
        name="local_products",
    )(ids, cotan, weight)


def fold_kernel(ids, owner, counts, acc, *refs, terms, parts, tile, first, blocks, slot, table_parts, held, final):
    p = pl.program_id(0)
    xs, refs = refs[:terms], refs[terms:]
    ws, refs = refs[: terms * parts], refs[terms * parts :]
    table, out = refs[:table_parts], refs[-1]
    _, flip = tile(first + p, ids)
    rows = lax.broadcasted_iota(jnp.int32, (BLK, PIECE), 0)

    def run(i):
        total = contract_last(xs[0][...], ws[i][...])
        for t in range(1, terms):
            total += contract_last(xs[t][...], ws[t * parts + i][...])
        for half in range(2):
            to = tile_part(half, flip)
            part = acc[:, to] + total[:, half * PIECE : (half + 1) * PIECE]
            if not final:
                out[:, to] = part
                continue
            for b in range(blocks):
                at = slice(b * BLK, (b + 1) * BLK)
                count = live_count(b, ids, owner, counts, blocks=blocks)
                out[at, to] = jnp.where(rows < count, part[at], 0.0).astype(BF)

    by_part(p, parts, run)
    if table:
        both = refs[table_parts]
        rank = both.shape[1] // 2
        for b in range(blocks):
            at = slice(b * BLK, (b + 1) * BLK)
            place = slot(b, ids, owner)
            for i, part in enumerate(table):

                @pl.when(place // held == i)
                def _(at=at, place=place, part=part):
                    out[at, :] += lax.dot_general(
                        both[at, rank:],
                        part[place % held],
                        (((1,), (0,)), ((), ())),
                        preferred_element_type=F32,
                    )


def fold(ids, owner, counts, acc, xs, ws, tile, first, *, blocks, owned, bits, before=None, final=False, table=(), both=None):
    tokens, width = acc.shape
    cols = xs[0].shape[1]
    parts = len(ws[0])
    flat = [part for w in ws for part in w]
    tiles = parts if parts > 1 else flat[0].shape[0] // TILE
    slot = functools.partial(slot_of, blocks=blocks, owned=owned, bits=bits)
    block = pl.BlockSpec((tokens, TILE), lambda p, i, *s: (0, tile(first + p, i)[0]))
    operands = [ids, owner, counts, acc, *xs, *flat, *table]
    in_specs = [block]
    in_specs += [pl.BlockSpec((tokens, cols), lambda p, *s: (0, 0)) for _ in xs]
    in_specs += [pl.BlockSpec((TILE, cols), lambda p, *s: (p if parts == 1 else 0, 0)) for _ in flat]
    held = 0
    if table:
        held, rank = table[0].shape[:2]
        in_specs += [
            pl.BlockSpec((held, rank, TILE), lambda p, i, *s: (0, 0, tile(first + p, i)[0])) for _ in table
        ]
        operands.append(both)
        in_specs.append(pl.BlockSpec((tokens, 2 * rank), lambda p, *s: (0, 0)))
    alias = {} if final else {3: 0}
    if before is not None:
        alias = {len(operands): 0}
        operands.append(before)
        in_specs.append(pl.BlockSpec(memory_space=pl.ANY))
    return pl.pallas_call(
        functools.partial(
            fold_kernel,
            terms=len(xs),
            parts=parts,
            tile=tile,
            first=first,
            blocks=blocks,
            slot=slot,
            table_parts=len(table),
            held=held,
            final=final,
        ),
        grid_spec=pltpu.PrefetchScalarGridSpec(
            num_scalar_prefetch=3, grid=(tiles,), in_specs=in_specs, out_specs=block
        ),
        out_shape=jax.ShapeDtypeStruct((tokens, width), BF if final else F32),
        input_output_aliases=alias,
        compiler_params=params(28),
        cost_estimate=CHEAP,
        name="finish" if final else "fold",
    )(*operands)


def line(cotan, n, z):
    ups, downs = [], []
    a = b = cotan
    for r in range(1, n):
        a = lax.ppermute(a, "tensor", [(i, i + 1) for i in range(r - 1, n - 1)])
        b = lax.ppermute(b, "tensor", [(i, i - 1) for i in range(n - r, 0, -1)])
        ups.append(a)
        downs.append(b)
    return [jnp.where(z >= s, ups[s - 1], downs[n - s - 1]) for s in range(1, n)]


def body(hidden, query_gradient, weight, down, up, owner, counts):
    n = lax.axis_size("tensor")
    nd = lax.axis_size("dp")
    ng = lax.axis_size("groups")
    x, me, z = lax.axis_index("groups"), lax.axis_index("dp"), lax.axis_index("tensor")
    middle = jnp.logical_and(z > 0, z < n - 1)
    ids = jnp.stack([x, me, z, middle.astype(jnp.int32)]).astype(jnp.int32)
    tokens, width = hidden.shape
    cols = query_gradient.shape[1]
    owned = down.shape[0]
    share = width // (ng * nd)
    bits = tuple(range(nd.bit_length() - 2, -1, -1))
    sizes = dict(blocks=tokens // BLK, owned=owned, bits=bits)
    fast = (ng, nd, n, share) == (2, 4, 4, PIECE)

    if fast:
        y, core = me // 2, me % 2
        place = jnp.where(core == 0, 2 * y + x, 4 + 2 * x + y)
        turn_a = [(i, i ^ (4 if i % 2 == 0 else 2)) for i in range(8)]
        turn_b = [(i, i ^ (2 if i % 2 == 0 else 4)) for i in range(8)]
        turn_c = [(i, i ^ 1) for i in range(8)]
        outer, inner = [(0, 1), (1, 0), (2, 3), (3, 2)], [(1, 2), (2, 1)]
        outward = [(1, 0), (2, 3)]
    else:
        place = x * nd + me
    copies = ("groups", "dp")

    def cut(to):
        return lax.dynamic_slice(weight, (to * width + place * share, 0), (share, cols))

    def piece(step, own):
        return move(f"piece{step}", own, "tensor", [(i, i ^ step) for i in range(n)])

    def turned(name, own, pairs):
        return jnp.concatenate([own, move(name, own, copies, pairs)], axis=0)

    def more(bit, parts):
        return parts + [
            (swap(f"down{bit}_{i}", down, "dp", nd, bit), swap(f"up{bit}_{i}", up, "dp", nd, bit))
            for i, (down, up) in enumerate(parts)
        ]

    def ranks(table):
        return rank_partials(ids, owner, counts, hidden, query_gradient, table, **sizes)

    def rank_sum(bit, both):
        got = swap(f"rank_sum{bit}", both, "tensor", n, bit)
        return (both.astype(F32) + got.astype(F32)).astype(BF)

    def grads(both):
        return member_grads(ids, owner, hidden, query_gradient, both, nd * owned, **sizes)

    def grad_sum(sends, keep):
        send = jnp.concatenate(sends, axis=0)
        for bit in reversed(bits):
            total = keep.astype(F32) + swap(f"grads{bit}", send, "dp", nd, bit).astype(F32)
            if bit != bits[0]:
                rest = total.shape[0] // 2
                keep, send = total[:rest], total[rest:].astype(BF)
        return jnp.swapaxes(total[:, :, :width], 1, 2), total[:, :, width:]

    def local():
        return local_products(ids, query_gradient, weight, width)

    def folded(acc, xs, ws, tile, first, **more):
        return fold(ids, owner, counts, acc, xs, ws, tile, first, **sizes, **more)

    if fast:
        piece1, piece3 = piece(1, cut(z ^ 1)), piece(3, cut(z ^ 3))
        table = more(bits[0], [(jnp.swapaxes(down, 1, 2), up)])
        cut2 = cut(z ^ 2)
        acc = local()
        piece1, piece3, cut2, table, acc = together(piece1, piece3, cut2, table, acc)

        by_one = move("outer", query_gradient, "tensor", outer)
        across = move("inner", query_gradient, "tensor", inner)
        near1 = move("turn_a1", piece1, copies, turn_a)
        near3 = move("turn_a3", piece3, copies, turn_a)
        table = more(bits[1], table)
        both = ranks(table)
        both = rank_sum(1, both)
        by_one, across, near1, near3, both, cut2 = together(by_one, across, near1, near3, both, cut2)
        wide1 = jnp.concatenate([piece1, near1], axis=0)
        wide3 = jnp.concatenate([piece3, near3], axis=0)

        half = tokens // 2
        one0, one1, over0, over1 = by_one[:half], by_one[half:], across[:half], across[half:]
        piece2 = piece(2, cut2)
        end_two0 = move("inner_out0", over0, "tensor", outward)
        wide1 = [wide1, move("turn_b1", wide1, copies, turn_b)]
        wide3 = [wide3, move("turn_b3", wide3, copies, turn_b)]
        both = rank_sum(0, both)
        sends, keep = grads(both)
        rest = len(sends) // 2
        one0, one1, over1, end_two0, piece2, wide1, wide3, sends = together(
            one0, one1, over1, end_two0, piece2, wide1, wide3, sends
        )

        end_two1 = move("inner_out1", over1, "tensor", outward)
        two0 = move("outer_in0", one0, "tensor", inner)
        two1 = move("outer_in1", one1, "tensor", inner)
        end_three0 = move("outer_in_out0", two0, "tensor", outward)
        wide2 = turned("turn_a2", piece2, turn_a)
        got = [swap(f"grads0_{i}", one, "dp", nd, bits[1]) for i, one in enumerate(sends)]
        far = keep[rest:].astype(F32) + jnp.concatenate(got[rest:], axis=0).astype(F32)
        far = swap("grads1", far.astype(BF), "dp", nd, bits[0])
        end_two1, two0, two1, end_three0, wide1, wide2, far = together(
            end_two1, two0, two1, end_three0, wide1, wide2, far
        )

        end_three1 = move("outer_in_out1", two1, "tensor", outward)
        wide2 = [wide2, move("turn_b2", wide2, copies, turn_b)]
        other1 = [move(f"turn_c1{i}", part, copies, turn_c) for i, part in enumerate(wide1)]
        acc = folded(acc, [by_one], [wide1 + other1], relative_tile, 0, table=[pair[0] for pair in table], both=both)
        two = jnp.where(
            middle, jnp.concatenate([two0, two1], axis=0), jnp.concatenate([end_two0, end_two1], axis=0)
        )
        total = keep[:rest].astype(F32) + jnp.concatenate(got[:rest], axis=0).astype(F32) + far.astype(F32)
        grad_down, grad_up = jnp.swapaxes(total[:, :, :width], 1, 2), total[:, :, width:]
        wide2, acc, end_three1, two, grad_down, grad_up = together(
            wide2, acc, end_three1, two, grad_down, grad_up
        )
        end_three = jnp.concatenate([end_three0, end_three1], axis=0)

        other2 = [move(f"turn_c2{i}", part, copies, turn_c) for i, part in enumerate(wide2)]
        other3 = [move(f"turn_c3{i}", part, copies, turn_c) for i, part in enumerate(wide3)]
        three = jnp.where(middle, across, end_three)
        result = folded(acc, [two, three], [wide2, wide3], relative_tile, 0, final=True)
        result = folded(acc, [two, three], [other2, other3], relative_tile, 2, before=result, final=True)
    else:
        table = [(jnp.swapaxes(down, 1, 2), up)]
        xs = line(query_gradient, n, z)
        wides = []
        for step in range(1, n):
            own = move(f"piece{step}", cut(lax.rem(z + step, n)), "tensor", [(i, (i + step) % n) for i in range(n)])
            wides.append((lax.all_gather(own, copies, axis=0, tiled=True),))
        for bit in bits:
            table = [tuple(jnp.concatenate(pair, axis=0) for pair in zip(*more(bit, table)))]
        both = ranks(table)
        for bit in range(n.bit_length() - 1):
            both = rank_sum(bit, both)
        grad_down, grad_up = grad_sum(*grads(both))
        acc = folded(local(), xs[:1], wides[:1], plain_tile, 0, table=[pair[0] for pair in table], both=both)
        result = folded(acc, xs[1:], wides[1:], plain_tile, 0, final=True)
    return result, grad_down, grad_up


def solution(mesh):
    return jax.shard_map(
        body,
        mesh=mesh,
        in_specs=(
            P(("groups", "dp"), "tensor"),
            P(("groups", "dp"), "tensor"),
            P(None, "tensor"),
            P(("groups", "dp"), "tensor", None),
            P(("groups", "dp"), None, "tensor"),
            P("groups"),
            P("groups"),
        ),
        out_specs=(
            P(("groups", "dp"), "tensor"),
            P(("groups", "dp"), "tensor", None),
            P(("groups", "dp"), None, "tensor"),
        ),
        check_vma=False,
    )
```

```python
import functools

import jax
import jax.numpy as jnp
from jax import lax
from jax.experimental import pallas as pl
from jax.experimental.pallas import tpu as pltpu
from jax.sharding import PartitionSpec as P

BLK = 128
PIECE = 256
TILE = 2 * PIECE
BF = jnp.bfloat16
F32 = jnp.float32


CHEAP = pl.CostEstimate(flops=1, bytes_accessed=1, transcendentals=0)


def move(name, a, axis, pairs):
    with jax.named_scope(name):
        return lax.ppermute(a, axis, pairs)


def swap(name, a, axis, size, bit):
    return move(name, a, axis, [(i, i ^ (1 << bit)) for i in range(size)])


def together(*values):
    return lax.optimization_barrier(values)


def contract_last(a, b):
    return lax.dot_general(a, b, (((1,), (1,)), ((), ())), preferred_element_type=F32)


def contract_first(a, b):
    return lax.dot_general(a, b, (((0,), (0,)), ((), ())), preferred_element_type=F32)


def params(mib):
    return pltpu.CompilerParams(vmem_limit_bytes=mib * 2**20)


def slot_of(block, ids, owner, *, blocks, owned, bits):
    member = owner[ids[1] * blocks + block]
    relative = (member // owned) ^ ids[1]
    slot = member % owned
    for j, bit in enumerate(bits):
        slot = slot + ((relative >> bit) & 1) * (owned << j)
    return slot


def live_count(block, ids, owner, counts, *, blocks):
    at = ids[1] * blocks + block
    last = owner.shape[0] - 1
    member = owner[at]
    closing = jnp.logical_or(at == last, owner[jnp.minimum(at + 1, last)] != member)
    return jnp.where(closing, counts[member], BLK)


def rank_kernel(ids, owner, counts, hid, cot, *refs, blocks, slot, held):
    b = pl.program_id(0)
    count = live_count(b, ids, owner, counts, blocks=blocks)
    parts, out = refs[:-1], refs[-1]
    for i in range(len(parts) // 2):

        @pl.when(slot(b, ids, owner) // held == i)
        def _(down=parts[2 * i], up=parts[2 * i + 1]):
            act = contract_last(hid[...], down[0])
            grad = contract_last(cot[...], up[0])
            both = jnp.concatenate([act, grad], axis=1)
            rows = lax.broadcasted_iota(jnp.int32, both.shape, 0)
            out[...] = jnp.where(rows < count, both, 0.0).astype(BF)


def rank_partials(ids, owner, counts, hidden, cotan, table, *, blocks, owned, bits):
    width, cols = hidden.shape[1], cotan.shape[1]
    held, rank = table[0][0].shape[:2]
    slot = functools.partial(slot_of, blocks=blocks, owned=owned, bits=bits)

    def chosen(i, size):
        def index(b, ids, owner, counts):
            at = slot(b, ids, owner)
            return (jnp.where(at // held == i, at % held, 0), 0, 0)

        return pl.BlockSpec((1, rank, size), index)

    return pl.pallas_call(
        functools.partial(rank_kernel, blocks=blocks, slot=slot, held=held),
        grid_spec=pltpu.PrefetchScalarGridSpec(
            num_scalar_prefetch=3,
            grid=(blocks,),
            in_specs=[
                pl.BlockSpec((BLK, width), lambda b, *s: (b, 0)),
                pl.BlockSpec((BLK, cols), lambda b, *s: (b, 0)),
            ]
            + [chosen(i, size) for i in range(len(table)) for size in (width, cols)],
            out_specs=pl.BlockSpec((BLK, 2 * rank), lambda b, *s: (b, 0)),
        ),
        out_shape=jax.ShapeDtypeStruct((blocks * BLK, 2 * rank), BF),
        compiler_params=params(16),
        cost_estimate=CHEAP,
        name="rank_partials",
    )(ids, owner, counts, hidden, cotan, *[one for pair in table for one in pair])


def grads_kernel(ids, owner, hid, cot, both, *refs, width, blocks, slot, half):
    sends, keep, acc = refs[:half], refs[half], refs[half + 1]
    step = pl.program_id(0)
    position = jnp.where(step < half, step + half, step - half)
    rank = both.shape[1] // 2
    acc[...] = jnp.zeros_like(acc)
    for b in range(blocks):

        @pl.when(slot(b, ids, owner) == position)
        def _(b=b):
            at = pl.ds(b * BLK, BLK)
            pair = both[at, :].astype(F32)
            acc[:, :width] += contract_first(pair[:, rank:].astype(BF), hid[at, :])
            acc[:, width:] += contract_first(pair[:, :rank].astype(BF), cot[at, :])

    for i, send in enumerate(sends):

        @pl.when(step == i)
        def _(send=send):
            send[0] = acc[...].astype(BF)

    @pl.when(step >= half)
    def _():
        keep[0] = acc[...].astype(BF)


def member_grads(ids, owner, hidden, cotan, both, members, *, blocks, owned, bits):
    tokens, width = hidden.shape
    cols = cotan.shape[1]
    rank = both.shape[1] // 2
    half = members // 2
    slot = functools.partial(slot_of, blocks=blocks, owned=owned, bits=bits)
    shape = lambda count: jax.ShapeDtypeStruct((count, rank, width + cols), BF)
    *sends, keep = pl.pallas_call(
        functools.partial(
            grads_kernel, width=width, blocks=blocks, slot=slot, half=half
        ),
        grid_spec=pltpu.PrefetchScalarGridSpec(
            num_scalar_prefetch=2,
            grid=(members,),
            in_specs=[
                pl.BlockSpec((tokens, width), lambda p, *s: (0, 0)),
                pl.BlockSpec((tokens, cols), lambda p, *s: (0, 0)),
                pl.BlockSpec((tokens, 2 * rank), lambda p, *s: (0, 0)),
            ],
            out_specs=[pl.BlockSpec((1, rank, width + cols), lambda p, *s: (0, 0, 0)) for _ in range(half)]
            + [pl.BlockSpec((1, rank, width + cols), lambda p, *s: (jnp.maximum(p - half, 0), 0, 0))],
            scratch_shapes=[pltpu.VMEM((rank, width + cols), F32)],
        ),
        out_shape=[shape(1)] * half + [shape(half)],
        compiler_params=params(16),
        cost_estimate=CHEAP,
        name="member_grads",
    )(ids, owner, hidden, cotan, both)
    return sends, keep


def relative_tile(p, ids):
    core = (ids[1] & 1) ^ (p >> 1)
    x, y = ids[0], (ids[1] >> 1) & 1
    at = jnp.where(core == 0, y ^ (p & 1), 2 + (x ^ (p & 1)))
    return at, jnp.where(core == 0, x, y)


def plain_tile(p, ids):
    return p, 0


def tile_part(half, flip):
    return pl.ds(pl.multiple_of((half ^ flip) * PIECE, PIECE), PIECE)


def by_part(p, parts, run):
    if parts == 1:
        run(0)
        return
    for i in range(parts):
        pl.when(p == i)(functools.partial(run, i))


def local_kernel(ids, cot, weight, out):
    out[...] = contract_last(cot[...], weight[...])


def local_products(ids, cotan, weight, width):
    tokens, cols = cotan.shape
    tiles = width // TILE
    return pl.pallas_call(
        local_kernel,
        grid_spec=pltpu.PrefetchScalarGridSpec(
            num_scalar_prefetch=1,
            grid=(tiles,),
            in_specs=[
                pl.BlockSpec((tokens, cols), lambda p, *s: (0, 0)),
                pl.BlockSpec((TILE, cols), lambda p, i: (i[2] * tiles + p, 0)),
            ],
            out_specs=pl.BlockSpec((tokens, TILE), lambda p, *s: (0, p)),
        ),
        out_shape=jax.ShapeDtypeStruct((tokens, width), F32),
        compiler_params=params(16),
        cost_estimate=CHEAP,
        name="local_products",
    )(ids, cotan, weight)


def fold_kernel(ids, owner, counts, acc, *refs, terms, parts, tile, first, blocks, slot, table_parts, held, final):
    p = pl.program_id(0)
    xs, refs = refs[:terms], refs[terms:]
    ws, refs = refs[: terms * parts], refs[terms * parts :]
    table, out = refs[:table_parts], refs[-1]
    _, flip = tile(first + p, ids)
    rows = lax.broadcasted_iota(jnp.int32, (BLK, PIECE), 0)

    def run(i):
        total = contract_last(xs[0][...], ws[i][...])
        for t in range(1, terms):
            total += contract_last(xs[t][...], ws[t * parts + i][...])
        for half in range(2):
            to = tile_part(half, flip)
            part = acc[:, to] + total[:, half * PIECE : (half + 1) * PIECE]
            if not final:
                out[:, to] = part
                continue
            for b in range(blocks):
                at = slice(b * BLK, (b + 1) * BLK)
                count = live_count(b, ids, owner, counts, blocks=blocks)
                out[at, to] = jnp.where(rows < count, part[at], 0.0).astype(BF)

    by_part(p, parts, run)
    if table:
        both = refs[table_parts]
        rank = both.shape[1] // 2
        for b in range(blocks):
            at = slice(b * BLK, (b + 1) * BLK)
            place = slot(b, ids, owner)
            for i, part in enumerate(table):

                @pl.when(place // held == i)
                def _(at=at, place=place, part=part):
                    out[at, :] += lax.dot_general(
                        both[at, rank:],
                        part[place % held],
                        (((1,), (0,)), ((), ())),
                        preferred_element_type=F32,
                    )


def fold(ids, owner, counts, acc, xs, ws, tile, first, *, blocks, owned, bits, before=None, final=False, table=(), both=None):
    tokens, width = acc.shape
    cols = xs[0].shape[1]
    parts = len(ws[0])
    flat = [part for w in ws for part in w]
    tiles = parts if parts > 1 else flat[0].shape[0] // TILE
    slot = functools.partial(slot_of, blocks=blocks, owned=owned, bits=bits)
    block = pl.BlockSpec((tokens, TILE), lambda p, i, *s: (0, tile(first + p, i)[0]))
    operands = [ids, owner, counts, acc, *xs, *flat, *table]
    in_specs = [block]
    in_specs += [pl.BlockSpec((tokens, cols), lambda p, *s: (0, 0)) for _ in xs]
    in_specs += [pl.BlockSpec((TILE, cols), lambda p, *s: (p if parts == 1 else 0, 0)) for _ in flat]
    held = 0
    if table:
        held, rank = table[0].shape[:2]
        in_specs += [
            pl.BlockSpec((held, rank, TILE), lambda p, i, *s: (0, 0, tile(first + p, i)[0])) for _ in table
        ]
        operands.append(both)
        in_specs.append(pl.BlockSpec((tokens, 2 * rank), lambda p, *s: (0, 0)))
    alias = {} if final else {3: 0}
    if before is not None:
        alias = {len(operands): 0}
        operands.append(before)
        in_specs.append(pl.BlockSpec(memory_space=pl.ANY))
    return pl.pallas_call(
        functools.partial(
            fold_kernel,
            terms=len(xs),
            parts=parts,
            tile=tile,
            first=first,
            blocks=blocks,
            slot=slot,
            table_parts=len(table),
            held=held,
            final=final,
        ),
        grid_spec=pltpu.PrefetchScalarGridSpec(
            num_scalar_prefetch=3, grid=(tiles,), in_specs=in_specs, out_specs=block
        ),
        out_shape=jax.ShapeDtypeStruct((tokens, width), BF if final else F32),
        input_output_aliases=alias,
        compiler_params=params(28),
        cost_estimate=CHEAP,
        name="finish" if final else "fold",
    )(*operands)


def line(cotan, n, z):
    ups, downs = [], []
    a = b = cotan
    for r in range(1, n):
        a = lax.ppermute(a, "tensor", [(i, i + 1) for i in range(r - 1, n - 1)])
        b = lax.ppermute(b, "tensor", [(i, i - 1) for i in range(n - r, 0, -1)])
        ups.append(a)
        downs.append(b)
    return [jnp.where(z >= s, ups[s - 1], downs[n - s - 1]) for s in range(1, n)]


def body(hidden, query_gradient, weight, down, up, owner, counts):
    n = lax.axis_size("tensor")
    nd = lax.axis_size("dp")
    ng = lax.axis_size("groups")
    x, me, z = lax.axis_index("groups"), lax.axis_index("dp"), lax.axis_index("tensor")
    middle = jnp.logical_and(z > 0, z < n - 1)
    ids = jnp.stack([x, me, z, middle.astype(jnp.int32)]).astype(jnp.int32)
    tokens, width = hidden.shape
    cols = query_gradient.shape[1]
    owned = down.shape[0]
    share = width // (ng * nd)
    bits = tuple(range(nd.bit_length() - 2, -1, -1))
    sizes = dict(blocks=tokens // BLK, owned=owned, bits=bits)
    fast = (ng, nd, n, share) == (2, 4, 4, PIECE)

    if fast:
        y, core = me // 2, me % 2
        place = jnp.where(core == 0, 2 * y + x, 4 + 2 * x + y)
        turn_a = [(i, i ^ (4 if i % 2 == 0 else 2)) for i in range(8)]
        turn_b = [(i, i ^ (2 if i % 2 == 0 else 4)) for i in range(8)]
        turn_c = [(i, i ^ 1) for i in range(8)]
        outer, inner = [(0, 1), (1, 0), (2, 3), (3, 2)], [(1, 2), (2, 1)]
        outward = [(1, 0), (2, 3)]
    else:
        place = x * nd + me
    copies = ("groups", "dp")

    def cut(to):
        return lax.dynamic_slice(weight, (to * width + place * share, 0), (share, cols))

    def piece(step, own):
        return move(f"piece{step}", own, "tensor", [(i, i ^ step) for i in range(n)])

    def turned(name, own, pairs):
        return jnp.concatenate([own, move(name, own, copies, pairs)], axis=0)

    def more(bit, parts):
        return parts + [
            (swap(f"down{bit}_{i}", down, "dp", nd, bit), swap(f"up{bit}_{i}", up, "dp", nd, bit))
            for i, (down, up) in enumerate(parts)
        ]

    def ranks(table):
        return rank_partials(ids, owner, counts, hidden, query_gradient, table, **sizes)

    def rank_sum(bit, both):
        got = swap(f"rank_sum{bit}", both, "tensor", n, bit)
        return (both.astype(F32) + got.astype(F32)).astype(BF)

    def grads(both):
        return member_grads(ids, owner, hidden, query_gradient, both, nd * owned, **sizes)

    def grad_sum(sends, keep):
        send = jnp.concatenate(sends, axis=0)
        for bit in reversed(bits):
            total = keep.astype(F32) + swap(f"grads{bit}", send, "dp", nd, bit).astype(F32)
            if bit != bits[0]:
                rest = total.shape[0] // 2
                keep, send = total[:rest], total[rest:].astype(BF)
        return jnp.swapaxes(total[:, :, :width], 1, 2), total[:, :, width:]

    def local():
        return local_products(ids, query_gradient, weight, width)

    def folded(acc, xs, ws, tile, first, **more):
        return fold(ids, owner, counts, acc, xs, ws, tile, first, **sizes, **more)

    if fast:
        piece1, piece3 = piece(1, cut(z ^ 1)), piece(3, cut(z ^ 3))
        table = more(bits[0], [(jnp.swapaxes(down, 1, 2), up)])
        cut2 = cut(z ^ 2)
        acc = local()
        piece1, piece3, cut2, table, acc = together(piece1, piece3, cut2, table, acc)

        by_one = move("outer", query_gradient, "tensor", outer)
        across = move("inner", query_gradient, "tensor", inner)
        near1 = move("turn_a1", piece1, copies, turn_a)
        near3 = move("turn_a3", piece3, copies, turn_a)
        table = more(bits[1], table)
        both = ranks(table)
        both = rank_sum(1, both)
        by_one, across, near1, near3, both, cut2 = together(by_one, across, near1, near3, both, cut2)
        wide1 = jnp.concatenate([piece1, near1], axis=0)
        wide3 = jnp.concatenate([piece3, near3], axis=0)

        half = tokens // 2
        one0, one1, over0, over1 = by_one[:half], by_one[half:], across[:half], across[half:]
        piece2 = piece(2, cut2)
        end_two0 = move("inner_out0", over0, "tensor", outward)
        wide1 = [wide1, move("turn_b1", wide1, copies, turn_b)]
        wide3 = [wide3, move("turn_b3", wide3, copies, turn_b)]
        both = rank_sum(0, both)
        sends, keep = grads(both)
        rest = len(sends) // 2
        one0, one1, over1, end_two0, piece2, wide1, wide3, sends = together(
            one0, one1, over1, end_two0, piece2, wide1, wide3, sends
        )

        end_two1 = move("inner_out1", over1, "tensor", outward)
        two0 = move("outer_in0", one0, "tensor", inner)
        two1 = move("outer_in1", one1, "tensor", inner)
        end_three0 = move("outer_in_out0", two0, "tensor", outward)
        wide2 = turned("turn_a2", piece2, turn_a)
        got = [swap(f"grads0_{i}", one, "dp", nd, bits[1]) for i, one in enumerate(sends)]
        far = keep[rest:].astype(F32) + jnp.concatenate(got[rest:], axis=0).astype(F32)
        far = swap("grads1", far.astype(BF), "dp", nd, bits[0])
        end_two1, two0, two1, end_three0, wide1, wide2, far = together(
            end_two1, two0, two1, end_three0, wide1, wide2, far
        )

        end_three1 = move("outer_in_out1", two1, "tensor", outward)
        core2 = move("turn_c20", wide2, copies, turn_c)
        wide2 = [wide2, move("turn_b2", wide2, copies, turn_b)]
        other1 = [move(f"turn_c1{i}", part, copies, turn_c) for i, part in enumerate(wide1)]
        acc = folded(acc, [by_one], [wide1 + other1], relative_tile, 0, table=[pair[0] for pair in table], both=both)
        two = jnp.where(
            middle, jnp.concatenate([two0, two1], axis=0), jnp.concatenate([end_two0, end_two1], axis=0)
        )
        total = keep[:rest].astype(F32) + jnp.concatenate(got[:rest], axis=0).astype(F32) + far.astype(F32)
        grad_down, grad_up = jnp.swapaxes(total[:, :, :width], 1, 2), total[:, :, width:]
        wide2, core2, acc, end_three1, two, grad_down, grad_up = together(
            wide2, core2, acc, end_three1, two, grad_down, grad_up
        )
        end_three = jnp.concatenate([end_three0, end_three1], axis=0)

        other2 = [core2, move("turn_c21", wide2[1], copies, turn_c)]
        other3 = [move(f"turn_c3{i}", part, copies, turn_c) for i, part in enumerate(wide3)]
        three = jnp.where(middle, across, end_three)
        result = folded(acc, [two, three], [wide2, wide3], relative_tile, 0, final=True)
        result = folded(acc, [two, three], [other2, other3], relative_tile, 2, before=result, final=True)
    else:
        table = [(jnp.swapaxes(down, 1, 2), up)]
        xs = line(query_gradient, n, z)
        wides = []
        for step in range(1, n):
            own = move(f"piece{step}", cut(lax.rem(z + step, n)), "tensor", [(i, (i + step) % n) for i in range(n)])
            wides.append((lax.all_gather(own, copies, axis=0, tiled=True),))
        for bit in bits:
            table = [tuple(jnp.concatenate(pair, axis=0) for pair in zip(*more(bit, table)))]
        both = ranks(table)
        for bit in range(n.bit_length() - 1):
            both = rank_sum(bit, both)
        grad_down, grad_up = grad_sum(*grads(both))
        acc = folded(local(), xs[:1], wides[:1], plain_tile, 0, table=[pair[0] for pair in table], both=both)
        result = folded(acc, xs[1:], wides[1:], plain_tile, 0, final=True)
    return result, grad_down, grad_up


def solution(mesh):
    return jax.shard_map(
        body,
        mesh=mesh,
        in_specs=(
            P(("groups", "dp"), "tensor"),
            P(("groups", "dp"), "tensor"),
            P(None, "tensor"),
            P(("groups", "dp"), "tensor", None),
            P(("groups", "dp"), None, "tensor"),
            P("groups"),
            P("groups"),
        ),
        out_specs=(
            P(("groups", "dp"), "tensor"),
            P(("groups", "dp"), "tensor", None),
            P(("groups", "dp"), None, "tensor"),
        ),
        check_vma=False,
    )
```
